32 devices in a mesh: col: 8 (over z, y), sec: 4 (over x, core).
Axes of the slice: x: 2, y: 2, z: 4, core: 2. Of those that a mesh axis runs over, the one named last changes fastest.
Arguments:
- transfer: float32 [16, 4, 256, 256], P('col', 'sec'), as said below
- hamiltonian: float32 [16, 3, 4, 256, 256], P('col', None, 'sec'), may hold values from -0.375 to 0.375
- kept: int32 [16, 4], P('col', 'sec'), may hold values from 128 to 256, as said below
Outputs:
- left_env: float32 [16, 4, 256, 256], P('col', 'sec')
- energy: float32 [16, 3], P('col')
The draws below stay inside these ranges and needn't reach their ends.
Inputs may be any that keep to these rules, and one draw needn't show every extreme that they name: Every kept dimension lies between half a sector and a whole sector, and some sector keeps all 256 states. `transfer`: each block is the identity plus an independent normal matrix of entries with deviation 0.2 / sqrt(256).
All inputs are finite; a program needn't handle non-finite values.
Results may differ from the reference program's by a relative error of at most 0.0003.
Values sent between devices are 32-bit elements; how exact they have to be, the bound alone decides.
No kernel may reach another device: no remote copies, remote signals or barrier semaphores. Data moves between devices by JAX's collectives and lax.ppermute only.
A program may use at most 64 MiB of HBM per device.

```python
import jax
import jax.numpy as jnp
from jax import lax

B = 256
TERMS = 3
NCOL = 16
NSEC = 4


def draw_transfer(key, part):
    noise = jax.random.normal(jax.random.fold_in(key, 11), (NCOL, NSEC, B, B), jnp.float32)
    eye = jnp.eye(B, dtype=jnp.float32)
    return eye[None, None, :, :] + noise * (0.2 / B ** 0.5)


def draw_kept(key, part):
    values = jax.random.randint(jax.random.fold_in(key, 21), (NCOL * NSEC,), B // 2, B + 1)
    spot = jax.random.randint(jax.random.fold_in(key, 22), (), 0, NCOL * NSEC)
    values = values.at[spot].set(B)
    return values.reshape(NCOL, NSEC).astype(jnp.int32)


def shard_levels(rng, dims, shards, least, top_value):
    gain = 1.0
    for dim, blocks in shards:
        heights = jax.random.uniform(jax.random.fold_in(jax.random.fold_in(rng, 6), dim), (blocks,), jnp.float32, least / len(shards), top_value / len(shards))
        gain = gain * jnp.repeat(jnp.exp(heights), dims[dim] // blocks).reshape((-1,) + (1,) * (len(dims) - 1 - dim))
    return gain


def normal_values(own_key, extent, deviation, most, cuts=(), kind=jnp.bfloat16):
    drawn = deviation * jax.random.normal(own_key, extent, jnp.float32)
    if cuts:
        drawn = drawn * shard_levels(own_key, extent, cuts, -0.22, 0.18)
    return jnp.clip(drawn, -most, most).astype(kind)


def setup_inputs(seed: int = 0) -> dict:
    key_list = jax.random.split(jax.random.key(seed), 4)
    return {
        "transfer": draw_transfer(jax.random.fold_in(key_list[3], 71), 0),
        "hamiltonian": normal_values(key_list[1], (NCOL, TERMS, NSEC, B, B), (1.0 / B ** 0.5), 0.375, ((0, 8), (2, 4)), jnp.float32),
        "kept": draw_kept(jax.random.fold_in(key_list[3], 71), 0),
    }


def one_sector(input_tensors):
    mats, kept_s, ham = input_tensors
    eye = jnp.eye(B, dtype=jnp.float32)

    def forward(acc, mat):
        return jnp.dot(acc, mat, precision=lax.Precision.HIGHEST), acc

    def backward(acc, mat):
        return jnp.dot(mat, acc, precision=lax.Precision.HIGHEST), acc

    whole, lefts = lax.scan(forward, eye, mats)
    unused, right_environments = lax.scan(backward, eye, mats, reverse=True)
    column_tensors = jnp.arange(B, dtype=jnp.int32)
    mask = (column_tensors[None, :] < kept_s[:, None]).astype(jnp.float32)
    masked = lefts * mask[:, None, :]
    inner_contraction = jnp.einsum("cji,jk->cik", masked, whole, precision=lax.Precision.HIGHEST)
    inner_contraction = jnp.einsum("fas,fms->fam", inner_contraction, right_environments, precision=lax.Precision.HIGHEST)
    partial_value = jnp.einsum("cil,ctil->ct", inner_contraction, ham, precision=lax.Precision.HIGHEST)
    norm = jnp.sum(whole * whole)
    return masked, partial_value, norm


def reference(transfer, hamiltonian, kept):
    mats = jnp.moveaxis(transfer, 1, 0)
    kept_t = jnp.moveaxis(kept, 1, 0)
    ham = jnp.moveaxis(hamiltonian, 2, 0)
    masked, partial_value, norm = lax.map(one_sector, (mats, kept_t, ham))
    left_env = jnp.moveaxis(masked, 0, 1)
    energy = (NSEC * B) * jnp.sum(partial_value, axis=0) / jnp.sum(norm)
    return left_env, energy
```

```python
import jax
import jax.numpy as jnp
from jax import lax
from jax.experimental import pallas as pl
from jax.experimental.pallas import tpu as pltpu
from jax.sharding import PartitionSpec as P

F32 = jnp.float32
BF16 = jnp.bfloat16
VMEM = pl.BlockSpec(memory_space=pltpu.VMEM)
SMEM = pl.BlockSpec(memory_space=pltpu.SMEM)
LIMIT = 40 * 1024 * 1024


def split(a):
    high = a.astype(BF16)
    return high, (a - high.astype(F32)).astype(BF16)


def dot(a, b, over):
    return lax.dot_general(a, b, ((over[0], over[1]), ((), ())), preferred_element_type=F32)


def multiply(a, b, over=((1,), (0,))):
    return dot(a[0], b[0], over) + (dot(a[0], b[1], over) + dot(a[1], b[0], over))


TN = ((0,), (0,))
NT = ((1,), (1,))


def group_kernel(transfer, out):
    out[...] = multiply(split(transfer[0, 0]), split(transfer[1, 0]))


def call(kernel, outs, in_specs, flops, *args):
    return pl.pallas_call(
        kernel,
        out_shape=outs,
        in_specs=in_specs,
        out_specs=jax.tree.map(lambda _: VMEM, outs),
        compiler_params=pltpu.CompilerParams(vmem_limit_bytes=LIMIT),
        cost_estimate=pl.CostEstimate(flops=flops, bytes_accessed=1 << 20, transcendentals=0),
    )(*args)


def eye(width):
    rows = lax.broadcasted_iota(jnp.int32, (width, width), 0)
    cols = lax.broadcasted_iota(jnp.int32, (width, width), 1)
    return jnp.where(rows == cols, 1.0, 0.0).astype(F32)


def quad_kernel(place, own, near, far, cross, sent, other_out):
    odd, high, upper = place[0] == 1, place[1] == 1, place[2] == 1
    own, near, far, cross = own[...], near[...], far[...], cross[...]
    mine = multiply(split(jnp.where(odd, near, own)), split(jnp.where(odd, own, near)))
    other = multiply(split(jnp.where(odd, cross, far)), split(jnp.where(odd, far, cross)))
    other_out[...] = other
    first = split(jnp.where(high, other, mine))
    second = split(jnp.where(high, mine, other))
    total = multiply(first, second)
    sent[...] = jnp.where(upper, total.T, total)


def shadow_kernel(place, kept, transfer, near, other, sent, hamiltonian, lefts_out, terms_out, norm_out):
    odd, high, upper = place[0] == 1, place[1] == 1, place[2] == 1
    width = near.shape[0]
    one = eye(width)
    near, other = near[...], other[...]
    left = multiply(split(jnp.where(high, other, one)), split(jnp.where(odd, near, one)))
    right = multiply(split(jnp.where(odd, one, near)), split(jnp.where(high, one, other)))
    lefts = [left, multiply(split(left), split(transfer[0, 0]))]
    rights = [multiply(split(transfer[1, 0]), split(right)), right]
    y = split(sent[...])
    norm_out[...] = multiply(y, y, TN)
    column = lax.broadcasted_iota(jnp.int32, (width, width), 1)
    for c in range(2):
        masked = jnp.where(column < kept[c, 0], lefts[c], 0.0)
        lefts_out[c] = masked
        a = jnp.where(upper, masked, multiply(y, split(masked), TN))
        b = jnp.where(upper, multiply(split(rights[c]), y), rights[c])
        a, b = split(a), split(b)
        for k in range(hamiltonian.shape[1]):
            inner = multiply(a, split(hamiltonian[c, k, 0]))
            terms_out[c, k] = multiply(split(inner), b)


def finish_kernel(x, terms, norm, out):
    x = split(x[...])
    z = multiply(x, x, TN)
    width = z.shape[0]
    rows = []
    for c in range(2):
        for k in range(terms.shape[1]):
            rows.append(jnp.sum(z * terms[c, k], axis=0, keepdims=True))
    rows.append(jnp.sum(z * norm[...], axis=0, keepdims=True))
    rows.append(jnp.zeros_like(rows[0]))
    table = jnp.concatenate(rows, axis=0)
    out[...] = table


def left_kernel(place, x, lefts, out):
    upper = place[2] == 1

    @pl.when(upper)
    def _():
        xs = split(x[...])
        for c in range(2):
            out[c, 0] = multiply(xs, split(lefts[c]))

    @pl.when(jnp.logical_not(upper))
    def _():
        for c in range(2):
            out[c, 0] = lefts[c]


def per_device(transfer, hamiltonian, kept):
    columns, width, terms = transfer.shape[0], transfer.shape[2], hamiltonian.shape[1]
    total = lax.axis_size("col")
    sectors = lax.axis_size("sec")
    place = lax.axis_index("col")
    bits = jnp.stack([place & 1, (place >> 1) & 1, place // (total // 2)]).astype(jnp.int32)
    matrix = jax.ShapeDtypeStruct((width, width), F32)
    one_product = 6 * width**3

    def swap(a, k):
        return lax.ppermute(a, "col", [(i, i ^ k) for i in range(total)])

    group = call(group_kernel, matrix, [VMEM], one_product, transfer)
    near, far, cross = swap(group, 1), swap(group, 2), swap(group, 3)
    sent, other = call(
        quad_kernel, (matrix, matrix), [SMEM] + [VMEM] * 4, 3 * one_product, bits, group, near, far, cross
    )
    x = swap(sent, total // 2)
    lefts, products, norm = call(
        shadow_kernel,
        (
            jax.ShapeDtypeStruct((columns, width, width), F32),
            jax.ShapeDtypeStruct((columns, terms, width, width), F32),
            matrix,
        ),
        [SMEM, SMEM] + [VMEM] * 5,
        24 * one_product,
        bits, kept, transfer, near, other, sent, hamiltonian,
    )
    table = call(
        finish_kernel, jax.ShapeDtypeStruct((8, width), F32), [VMEM] * 3, 2 * one_product, x, products, norm
    )
    parts = [table] + [lax.ppermute(table, "sec", [(i, i ^ k) for i in range(sectors)]) for k in range(1, sectors)]
    left_env = call(
        left_kernel, jax.ShapeDtypeStruct((columns, 1, width, width), F32), [SMEM, VMEM, VMEM], 2 * one_product,
        bits, x, lefts,
    )
    while len(parts) > 1:
        parts = [a + b for a, b in zip(parts[::2], parts[1::2])]
    sums = jnp.sum(parts[0], axis=1)
    scale = float(width * sectors)
    energy = scale * sums[:6].reshape(columns, terms) / sums[6]
    return left_env, energy


def solution(mesh):
    in_specs = (P("col", "sec", None, None), P("col", None, "sec", None, None), P("col", "sec"))
    out_specs = (P("col", "sec", None, None), P("col", None))
    return jax.shard_map(
        per_device, mesh=mesh, in_specs=in_specs, out_specs=out_specs, check_vma=False
    )
```

```python
import jax
import jax.numpy as jnp
from jax import lax
from jax.experimental import pallas as pl
from jax.experimental.pallas import tpu as pltpu
from jax.sharding import PartitionSpec as P

F32 = jnp.float32
BF16 = jnp.bfloat16
VMEM = pl.BlockSpec(memory_space=pltpu.VMEM)
SMEM = pl.BlockSpec(memory_space=pltpu.SMEM)
LIMIT = 40 * 1024 * 1024
LANES = 128
TN = ((0,), (0,))


def split(a):
    high = a.astype(BF16)
    return high, (a - high.astype(F32)).astype(BF16)


def dot(a, b, over):
    return lax.dot_general(a, b, (over, ((), ())), preferred_element_type=F32)


def multiply(a, b, over=((1,), (0,))):
    return dot(a[0], b[0], over) + (dot(a[0], b[1], over) + dot(a[1], b[0], over))


def product(a, b):
    return multiply(split(a), split(b))


def bit(k):
    return (lax.axis_index("col") // k) % 2 == 1


def eye(width):
    rows = lax.broadcasted_iota(jnp.int32, (width, width), 0)
    return (rows == lax.broadcasted_iota(jnp.int32, (width, width), 1)).astype(F32)


def group_kernel(transfer, out):
    out[...] = product(transfer[0, 0], transfer[1, 0])


def quad_kernel(own, near, far, cross, whole, other_out):
    odd, high = bit(1), bit(2)
    own, near, far, cross = own[...], near[...], far[...], cross[...]
    mine = product(jnp.where(odd, near, own), jnp.where(odd, own, near))
    other = product(jnp.where(odd, cross, far), jnp.where(odd, far, cross))
    other_out[...] = other
    whole[...] = product(jnp.where(high, other, mine), jnp.where(high, mine, other))


def sides_kernel(near, other, left_out, right_out):
    odd, high = bit(1), bit(2)
    near, other = near[...], other[...]
    one = eye(near.shape[0])
    left_out[...] = product(jnp.where(high, other, one), jnp.where(odd, near, one))
    right_out[...] = product(jnp.where(odd, one, near), jnp.where(high, one, other))


def level_kernel(k, whole, left, right, x, whole_out, left_out, right_out):
    after = bit(k)
    whole, left, right, x = whole[...], left[...], right[...], x[...]
    one = eye(whole.shape[0])
    whole_out[...] = product(jnp.where(after, x, whole), jnp.where(after, whole, x))
    left_out[...] = product(jnp.where(after, x, one), left)
    right_out[...] = product(right, jnp.where(after, one, x))


def shares_kernel(k, whole, sent, share, rest):
    @pl.when(bit(k))
    def _():
        sent[...] = whole[...].T

    @pl.when(jnp.logical_not(bit(k)))
    def _():
        sent[...] = whole[...]

    rows = share.shape[0]
    share[...] = sent[pl.ds(pl.multiple_of(bit(1).astype(jnp.int32) * rows, rows), rows)]
    rest[...] = sent[2 * rows :]


def terms_kernel(k, kept, transfer, left, right, sent, hamiltonian, lefts_out, terms_out, norm_out):
    upper = bit(k)
    columns, terms, width = terms_out.shape[0], terms_out.shape[1], left.shape[0]
    lefts = [left[...], product(left[...], transfer[0, 0])]
    rights = [product(transfer[1, 0], right[...]), right[...]]
    y = split(sent[...])
    norm_out[...] = multiply(y, y, TN)
    column = lax.broadcasted_iota(jnp.int32, (width, width), 1)
    for c in range(columns):
        masked = jnp.where(column < kept[c, 0], lefts[c], 0.0)
        lefts_out[c] = masked
        a = split(jnp.where(upper, masked, multiply(y, split(masked), TN)))
        b = split(jnp.where(upper, multiply(split(rights[c]), y), rights[c]))
        for t in range(terms):
            inner = multiply(a, split(hamiltonian[c, t, 0]))
            terms_out[c, t] = multiply(split(inner), b)


def finish_kernel(share, swapped, rest, terms, norm, out, x):
    rows = share.shape[0]
    at = bit(1).astype(jnp.int32) * rows
    x[pl.ds(pl.multiple_of(at, rows), rows)] = share[...]
    x[pl.ds(pl.multiple_of(rows - at, rows), rows)] = swapped[...]
    x[2 * rows :] = rest[...]
    xs = split(x[...])
    z = multiply(xs, xs, TN)
    columns, count = terms.shape[0], terms.shape[1]

    def total(m):
        s = jnp.sum(z * m, axis=0, keepdims=True)
        return sum(s[:, i : i + LANES] for i in range(0, s.shape[1], LANES))

    sums = [total(terms[c, t]) for c in range(columns) for t in range(count)] + [total(norm[...])]
    sums += [jnp.zeros_like(sums[0])] * (out.shape[0] - len(sums))
    out[...] = jnp.concatenate(sums, axis=0)


def left_kernel(k, x, lefts, out):
    @pl.when(bit(k))
    def _():
        xs = split(x[...])
        for c in range(out.shape[0]):
            out[c, 0] = multiply(xs, split(lefts[c]))

    @pl.when(jnp.logical_not(bit(k)))
    def _():
        out[:, 0] = lefts[...]


def energy_kernel(scale, *refs):
    parts, out = [r[...] for r in refs[:-1]], refs[-1]
    while len(parts) > 1:
        parts = [a + b for a, b in zip(parts[::2], parts[1::2])]
    columns, terms = out.shape
    s = jnp.sum(parts[0], axis=1, keepdims=True)
    s = jnp.broadcast_to(scale * s / s[columns * terms : columns * terms + 1], parts[0].shape)
    row = lax.broadcasted_iota(jnp.int32, s.shape, 0)
    lane = lax.broadcasted_iota(jnp.int32, s.shape, 1)
    for c in range(columns):
        out[c : c + 1] = jnp.sum(jnp.where(row == c * terms + lane, s, 0.0), axis=0, keepdims=True)[:, :terms]


def call(kernel, outs, flops, *args, smem=0):
    return pl.pallas_call(
        kernel,
        out_shape=outs,
        in_specs=[SMEM] * smem + [VMEM] * (len(args) - smem),
        out_specs=jax.tree.map(lambda _: VMEM, outs),
        compiler_params=pltpu.CompilerParams(vmem_limit_bytes=LIMIT),
        cost_estimate=pl.CostEstimate(flops=flops, bytes_accessed=1 << 20, transcendentals=0),
    )(*args)


def per_device(transfer, hamiltonian, kept):
    columns, width, terms = transfer.shape[0], transfer.shape[2], hamiltonian.shape[1]
    total, sectors = lax.axis_size("col"), lax.axis_size("sec")
    half = total // 2
    one = 6 * width**3

    def array(*shape):
        return jax.ShapeDtypeStruct(shape, F32)

    matrix = array(width, width)

    def swap(a, k):
        return lax.ppermute(a, "col", [(i, i ^ k) for i in range(total)])

    group = call(group_kernel, matrix, one, transfer)
    near, far, cross = swap(group, 1), swap(group, 2), swap(group, 3)
    whole, other = call(quad_kernel, (matrix, matrix), 3 * one, group, near, far, cross)
    if total > 8:
        left, right = call(sides_kernel, (matrix, matrix), 2 * one, near, other)
        k = 4
        while k < half:
            x = swap(whole, k)
            whole, left, right = call(
                lambda *refs, k=k: level_kernel(k, *refs), (matrix,) * 3, 3 * one, whole, left, right, x
            )
            k *= 2
    rows = width // 4
    sent, share, rest = call(
        lambda *refs: shares_kernel(half, *refs), (matrix, array(rows, width), array(width - 2 * rows, width)), one, whole
    )
    share = swap(share, half)
    rest = swap(rest, half)
    swapped = swap(share, 1)
    if total <= 8:
        left, right = call(sides_kernel, (matrix, matrix), 2 * one, near, other)
    lefts, products, norm = call(
        lambda *refs: terms_kernel(half, *refs),
        (array(columns, width, width), array(columns, terms, width, width), matrix),
        24 * one,
        kept, transfer, left, right, sent, hamiltonian,
        smem=1,
    )
    table_rows = -(-(columns * terms + 1) // 8) * 8
    table, x = call(
        finish_kernel, (array(table_rows, LANES), matrix), 2 * one, share, swapped, rest, products, norm
    )
    parts = [table] + [lax.ppermute(table, "sec", [(i, i ^ k) for i in range(sectors)]) for k in range(1, sectors)]
    left_env = call(
        lambda *refs: left_kernel(half, *refs), array(columns, 1, width, width), 2 * one, x, lefts
    )
    scale = float(width * sectors)
    energy = call(lambda *refs: energy_kernel(scale, *refs), array(columns, terms), 1000, *parts)
    return left_env, energy


def solution(mesh):
    in_specs = (P("col", "sec", None, None), P("col", None, "sec", None, None), P("col", "sec"))
    out_specs = (P("col", "sec", None, None), P("col", None))
    return jax.shard_map(
        per_device, mesh=mesh, in_specs=in_specs, out_specs=out_specs, check_vma=False
    )
```

```python
import jax
import jax.numpy as jnp
from jax import lax
from jax.experimental import pallas as pl
from jax.experimental.pallas import tpu as pltpu
from jax.sharding import PartitionSpec as P

F32 = jnp.float32
BF16 = jnp.bfloat16
VMEM = pl.BlockSpec(memory_space=pltpu.VMEM)
SMEM = pl.BlockSpec(memory_space=pltpu.SMEM)
LIMIT = 40 * 1024 * 1024
LANES = 128
FIRST = 10
TN = ((0,), (0,))


def split(a):
    high = a.astype(BF16)
    return high, (a - high.astype(F32)).astype(BF16)


def dot(a, b, over):
    return lax.dot_general(a, b, (over, ((), ())), preferred_element_type=F32)


def multiply(a, b, over=((1,), (0,))):
    return dot(a[0], b[0], over) + (dot(a[0], b[1], over) + dot(a[1], b[0], over))


def product(a, b):
    return multiply(split(a), split(b))


def bit(k):
    return (lax.axis_index("col") // k) % 2 == 1


def eye(width):
    rows = lax.broadcasted_iota(jnp.int32, (width, width), 0)
    return (rows == lax.broadcasted_iota(jnp.int32, (width, width), 1)).astype(F32)


def group_kernel(transfer, whole, *parts):
    group = product(transfer[0, 0], transfer[1, 0])

    @pl.when(bit(1))
    def _():
        whole[...] = group.T

    @pl.when(jnp.logical_not(bit(1)))
    def _():
        whole[...] = group

    at = 0
    for part in parts:
        part[...] = whole[at : at + part.shape[0]]
        at += part.shape[0]


def pair_kernel(near, own, out):
    out[...] = multiply(split(near[...]), split(own[...]), ((1,), (1,)))


def whole_of(parts):
    return jnp.concatenate([part[...] for part in parts], axis=0)


def begin_kernel(n, *refs):
    pairs, fars, out = refs[:n], refs[n:-1], refs[-1]
    pair, far = whole_of(pairs), whole_of(fars)
    rows = far.shape[0]

    @pl.when(bit(1) == bit(2))
    def _():
        out[:rows] = product(far, pair)
        out[rows:] = jnp.zeros_like(out[rows:])

    @pl.when(bit(1) != bit(2))
    def _():
        out[...] = product(pair[:, :rows], far)


def end_quad(begun, pairs, far, room):
    pair, far = whole_of(pairs), far[...]
    at = pair.shape[0] - far.shape[0]

    @pl.when(bit(1) == bit(2))
    def _():
        room[:at] = begun[:at]
        room[at:] = product(far, pair)

    @pl.when(bit(1) != bit(2))
    def _():
        room[...] = begun[...] + product(pair[:, at:], far)

    return room[...]


def quad_kernel(n, begun, *refs):
    pairs, (far, whole, room) = refs[:n], refs[n:]
    value = end_quad(begun, pairs, far, room)
    whole[...] = jnp.where(bit(1), value, value.T)


def spread(value, flip, sent, share, rest):
    @pl.when(flip)
    def _():
        sent[...] = value.T

    @pl.when(jnp.logical_not(flip))
    def _():
        sent[...] = value

    rows = share.shape[0]
    share[...] = sent[pl.ds(pl.multiple_of(bit(1).astype(jnp.int32) * rows, rows), rows)]
    rest[...] = sent[2 * rows :]


def quad_shares_kernel(n, k, begun, *refs):
    pairs, (far, sent, share, rest, room) = refs[:n], refs[n:]
    spread(end_quad(begun, pairs, far, room), bit(1) == bit(k), sent, share, rest)


def shares_kernel(k, whole, sent, share, rest):
    spread(whole[...], bit(k), sent, share, rest)


def sides(nears, fars):
    odd, high = bit(1), bit(2)
    near, other = whole_of(nears), whole_of(fars)
    near, other = jnp.where(odd, near, near.T), jnp.where(odd, other, other.T)
    one = eye(near.shape[0])
    left = product(jnp.where(high, other, one), jnp.where(odd, near, one))
    right = product(jnp.where(odd, one, near), jnp.where(high, one, other))
    return left, right


def sides_kernel(n, *refs):
    refs[2 * n][...], refs[2 * n + 1][...] = sides(refs[:n], refs[n : 2 * n])


def level_kernel(k, whole, left, right, x, whole_out, left_out, right_out):
    after = bit(k)
    whole, left, right, x = whole[...], left[...], right[...], x[...]
    one = eye(whole.shape[0])
    whole_out[...] = product(jnp.where(after, x, whole), jnp.where(after, whole, x))
    left_out[...] = product(jnp.where(after, x, one), left)
    right_out[...] = product(right, jnp.where(after, one, x))


def prepare(k, kept, transfer, left, right, sent, lefts_out, norm_out, a_out, b_out):
    upper = bit(k)
    width = left.shape[0]
    lefts = [left, product(left, transfer[0, 0])]
    rights = [product(transfer[1, 0], right), right]
    y = split(sent[...])
    norm_out[...] = multiply(y, y, TN)
    column = lax.broadcasted_iota(jnp.int32, (width, width), 1)
    for c in range(len(lefts)):
        masked = jnp.where(column < kept[c, 0], lefts[c], 0.0)
        lefts_out[c] = masked
        a_out[c, 0], a_out[c, 1] = split(jnp.where(upper, masked, multiply(y, split(masked), TN)))
        b_out[c, 0], b_out[c, 1] = split(jnp.where(upper, multiply(split(rights[c]), y), rights[c]))


def prepare_quad_kernel(n, k, kept, transfer, sent, *refs):
    left, right = sides(refs[:n], refs[n : 2 * n])
    prepare(k, kept, transfer, left, right, sent, *refs[2 * n :])


def prepare_kernel(k, kept, transfer, sent, left, right, *outs):
    prepare(k, kept, transfer, left[...], right[...], sent, *outs)


def terms_kernel(a, b, hamiltonian, out):
    for c in range(out.shape[0]):
        for t in range(out.shape[1]):
            inner = multiply((a[c, 0], a[c, 1]), split(hamiltonian[c, t, 0]))
            out[c, t] = multiply(split(inner), (b[c, 0], b[c, 1]))


def finish_kernel(share, swapped, rest, terms, norm, out, x):
    rows = share.shape[0]
    at = bit(1).astype(jnp.int32) * rows
    x[pl.ds(pl.multiple_of(at, rows), rows)] = share[...]
    x[pl.ds(pl.multiple_of(rows - at, rows), rows)] = swapped[...]
    x[2 * rows :] = rest[...]
    xs = split(x[...])
    z = multiply(xs, xs, TN)
    columns, count = terms.shape[0], terms.shape[1]

    def total(m):
        s = jnp.sum(z * m, axis=0, keepdims=True)
        return sum(s[:, i : i + LANES] for i in range(0, s.shape[1], LANES))

    sums = [total(terms[c, t]) for c in range(columns) for t in range(count)] + [total(norm[...])]
    sums += [jnp.zeros_like(sums[0])] * (out.shape[0] - len(sums))
    out[...] = jnp.concatenate(sums, axis=0)


def left_kernel(k, x, lefts, out):
    @pl.when(bit(k))
    def _():
        xs = split(x[...])
        for c in range(out.shape[0]):
            out[c, 0] = multiply(xs, split(lefts[c]))

    @pl.when(jnp.logical_not(bit(k)))
    def _():
        out[:, 0] = lefts[...]


def energy_kernel(scale, *refs):
    parts, out = [r[...] for r in refs[:-1]], refs[-1]
    while len(parts) > 1:
        parts = [a + b for a, b in zip(parts[::2], parts[1::2])]
    columns, terms = out.shape
    s = jnp.sum(parts[0], axis=1, keepdims=True)
    s = jnp.broadcast_to(scale * s / s[columns * terms : columns * terms + 1], parts[0].shape)
    row = lax.broadcasted_iota(jnp.int32, s.shape, 0)
    lane = lax.broadcasted_iota(jnp.int32, s.shape, 1)
    for c in range(columns):
        out[c : c + 1] = jnp.sum(jnp.where(row == c * terms + lane, s, 0.0), axis=0, keepdims=True)[:, :terms]


def call(kernel, outs, flops, *args, smem=0, scratch=()):
    return pl.pallas_call(
        kernel,
        out_shape=outs,
        in_specs=[SMEM] * smem + [VMEM] * (len(args) - smem),
        out_specs=jax.tree.map(lambda _: VMEM, outs),
        scratch_shapes=list(scratch),
        compiler_params=pltpu.CompilerParams(vmem_limit_bytes=LIMIT),
        cost_estimate=pl.CostEstimate(flops=flops, bytes_accessed=1 << 20, transcendentals=0),
    )(*args)


def per_device(transfer, hamiltonian, kept):
    columns, width, terms = transfer.shape[0], transfer.shape[2], hamiltonian.shape[1]
    total, sectors = lax.axis_size("col"), lax.axis_size("sec")
    half = total // 2
    one = 6 * width**3

    def array(*shape, dtype=F32):
        return jax.ShapeDtypeStruct(shape, dtype)

    matrix = array(width, width)
    room = (pltpu.VMEM((width, width), F32),)

    def swap(a, k):
        return lax.ppermute(a, "col", [(i, i ^ k) for i in range(total)])

    first = width * FIRST // 16
    heights = (first, width - first)
    n = len(heights)
    own, *parts = call(group_kernel, (matrix,) + tuple(array(h, width) for h in heights), one, transfer)
    nears = [swap(part, 1) for part in parts]
    pairs, fars = [], []
    for near, h in zip(nears, heights):
        pairs.append(call(pair_kernel, array(h, width), one // n, near, own))
        fars.append(swap(pairs[-1], 2))
    begun = call(lambda *refs: begin_kernel(n, *refs), matrix, one, *pairs, *fars[:-1])
    rows = width // 4
    shared = (matrix, array(rows, width), array(width - 2 * rows, width))
    if total <= 8:
        sent, share, rest = call(
            lambda *refs: quad_shares_kernel(n, half, *refs), shared, one, begun, *pairs, fars[-1], scratch=room
        )
    else:
        whole = call(lambda *refs: quad_kernel(n, *refs), matrix, one, begun, *pairs, fars[-1], scratch=room)
        left, right = call(lambda *refs: sides_kernel(n, *refs), (matrix, matrix), 2 * one, *nears, *fars)
        k = 4
        while k < half:
            x = swap(whole, k)
            whole, left, right = call(
                lambda *refs, k=k: level_kernel(k, *refs), (matrix,) * 3, 3 * one, whole, left, right, x
            )
            k *= 2
        sent, share, rest = call(lambda *refs: shares_kernel(half, *refs), shared, one, whole)
    share = swap(share, half)
    rest = swap(rest, half)
    halves = array(columns, 2, width, width, dtype=BF16)
    prepared = (array(columns, width, width), matrix, halves, halves)
    if total <= 8:
        lefts, norm, a, b = call(
            lambda *refs: prepare_quad_kernel(n, half, *refs), prepared, 9 * one, kept, transfer, sent, *nears, *fars,
            smem=1,
        )
    else:
        lefts, norm, a, b = call(
            lambda *refs: prepare_kernel(half, *refs), prepared, 9 * one, kept, transfer, sent, left, right, smem=1
        )
    share, norm = lax.optimization_barrier((share, norm))
    swapped = swap(share, 1)
    products = call(terms_kernel, array(columns, terms, width, width), 12 * one, a, b, hamiltonian)
    table_rows = -(-(columns * terms + 1) // 8) * 8
    table, x = call(
        finish_kernel, (array(table_rows, LANES), matrix), 2 * one, share, swapped, rest, products, norm
    )
    parts = [table] + [lax.ppermute(table, "sec", [(i, i ^ k) for i in range(sectors)]) for k in range(1, sectors)]
    left_env = call(
        lambda *refs: left_kernel(half, *refs), array(columns, 1, width, width), 2 * one, x, lefts
    )
    scale = float(width * sectors)
    energy = call(lambda *refs: energy_kernel(scale, *refs), array(columns, terms), 1000, *parts)
    return left_env, energy


def solution(mesh):
    in_specs = (P("col", "sec", None, None), P("col", None, "sec", None, None), P("col", "sec"))
    out_specs = (P("col", "sec", None, None), P("col", None))
    return jax.shard_map(
        per_device, mesh=mesh, in_specs=in_specs, out_specs=out_specs, check_vma=False
    )
```

```python
import jax
import jax.numpy as jnp
from jax import lax
from jax.experimental import pallas as pl
from jax.experimental.pallas import tpu as pltpu
from jax.sharding import PartitionSpec as P

F32 = jnp.float32
BF16 = jnp.bfloat16
VMEM = pl.BlockSpec(memory_space=pltpu.VMEM)
SMEM = pl.BlockSpec(memory_space=pltpu.SMEM)
LIMIT = 40 * 1024 * 1024
LANES = 128
FIRST = (21, 11)
SHARE = 10


def split(a):
    high = a.astype(BF16)
    return high, (a - high.astype(F32)).astype(BF16)


def dot(a, b, over):
    return lax.dot_general(a, b, (over, ((), ())), preferred_element_type=F32)


def multiply(a, b, over=((1,), (0,))):
    return dot(a[0], b[0], over) + (dot(a[0], b[1], over) + dot(a[1], b[0], over))


def product(a, b):
    return multiply(split(a), split(b))


def bit(k):
    return (lax.axis_index("col") // k) % 2 == 1


def eye(width):
    rows = lax.broadcasted_iota(jnp.int32, (width, width), 0)
    return (rows == lax.broadcasted_iota(jnp.int32, (width, width), 1)).astype(F32)


def group_kernel(transfer, whole, *parts):
    group = product(transfer[0, 0], transfer[1, 0])

    @pl.when(bit(1))
    def _():
        whole[...] = group.T

    @pl.when(jnp.logical_not(bit(1)))
    def _():
        whole[...] = group

    at = 0
    for part in parts:
        part[...] = whole[at : at + part.shape[0]]
        at += part.shape[0]


def pair_kernel(near, own, out):
    out[...] = multiply(split(near[...]), split(own[...]), ((1,), (1,)))


def whole_of(parts):
    return jnp.concatenate([part[...] for part in parts], axis=0)


def begin_kernel(n, *refs):
    pairs, fars, out = refs[:n], refs[n:-1], refs[-1]
    pair, far = whole_of(pairs), whole_of(fars)
    rows = far.shape[0]

    @pl.when(bit(1) == bit(2))
    def _():
        out[:rows] = product(far, pair)
        out[rows:] = jnp.zeros_like(out[rows:])

    @pl.when(bit(1) != bit(2))
    def _():
        out[...] = product(pair[:, :rows], far)


def end_quad(begun, pairs, far, room):
    pair, far = whole_of(pairs), far[...]
    at = pair.shape[0] - far.shape[0]

    @pl.when(bit(1) == bit(2))
    def _():
        room[:at] = begun[:at]
        room[at:] = product(far, pair)

    @pl.when(bit(1) != bit(2))
    def _():
        room[...] = begun[...] + product(pair[:, at:], far)

    return room[...]


def quad_kernel(n, begun, *refs):
    pairs, (far, whole, room) = refs[:n], refs[n:]
    value = end_quad(begun, pairs, far, room)
    whole[...] = jnp.where(bit(1), value, value.T)


def spread(value, flip, sent, share, rest):
    @pl.when(flip)
    def _():
        sent[...] = value.T

    @pl.when(jnp.logical_not(flip))
    def _():
        sent[...] = value

    rows = share.shape[0]
    share[...] = sent[pl.ds(pl.multiple_of(bit(1).astype(jnp.int32) * rows, 8), rows)]
    rest[...] = sent[2 * rows :]


def quad_sent_kernel(n, k, begun, *refs):
    pairs, (far, sent, share, rest, room) = refs[:n], refs[n:]
    spread(end_quad(begun, pairs, far, room), bit(1) == bit(k), sent, share, rest)


def sent_kernel(k, whole, sent, share, rest):
    spread(whole[...], bit(k), sent, share, rest)


def near_kernel(n, transfer, *refs):
    nears, (left, right) = refs[:n], refs[n:]
    odd = bit(1)
    near = whole_of(nears)

    @pl.when(odd)
    def _():
        left[0] = near
        left[1] = product(near, transfer[0, 0])
        right[0] = transfer[1, 0]
        right[1] = eye(near.shape[0])

    @pl.when(jnp.logical_not(odd))
    def _():
        value = near.T
        left[0] = eye(near.shape[0])
        left[1] = transfer[0, 0]
        right[0] = product(transfer[1, 0], value)
        right[1] = value


def sides(left, right, fars, lefts, rights):
    high = bit(2)
    other = whole_of(fars)
    other = split(jnp.where(bit(1), other, other.T))

    @pl.when(high)
    def _():
        rights[...] = right[...]
        for c in range(lefts.shape[0]):
            lefts[c] = multiply(other, split(left[c]))

    @pl.when(jnp.logical_not(high))
    def _():
        lefts[...] = left[...]
        for c in range(lefts.shape[0]):
            rights[c] = multiply(split(right[c]), other)


def sides_kernel(n, left, right, *refs):
    sides(left, right, refs[:n], *refs[n:])


def level_kernel(k, whole, left, right, x, whole_out, left_out, right_out):
    after = bit(k)
    whole, left, right, x = whole[...], left[...], right[...], x[...]
    one = eye(whole.shape[0])
    whole_out[...] = product(jnp.where(after, x, whole), jnp.where(after, whole, x))
    for c in range(left.shape[0]):
        left_out[c] = product(jnp.where(after, x, one), left[c])
        right_out[c] = product(right[c], jnp.where(after, one, x))


def prepare(k, kept, sent, lefts, rights, lefts_out, norm_out, a_out, b_out):
    y, transposed = split(sent[...]), split(sent[...].T)
    norm_out[...] = multiply(transposed, y)
    column = lax.broadcasted_iota(jnp.int32, lefts.shape[1:], 1)
    for c in range(lefts.shape[0]):
        lefts_out[c] = jnp.where(column < kept[c : c + 1], lefts[c], 0.0)

    @pl.when(bit(k))
    def _():
        for c in range(lefts.shape[0]):
            a_out[c, 0], a_out[c, 1] = split(lefts_out[c])
            b_out[c, 0], b_out[c, 1] = split(multiply(split(rights[c]), y))

    @pl.when(jnp.logical_not(bit(k)))
    def _():
        for c in range(lefts.shape[0]):
            a_out[c, 0], a_out[c, 1] = split(multiply(transposed, split(lefts_out[c])))
            b_out[c, 0], b_out[c, 1] = split(rights[c])


def prepare_quad_kernel(n, k, kept, sent, left, right, *refs):
    fars, outs, (lefts, rights) = refs[:n], refs[n:-2], refs[-2:]
    sides(left, right, fars, lefts, rights)
    prepare(k, kept, sent, lefts, rights, *outs)


def prepare_kernel(k, kept, sent, lefts, rights, *outs):
    prepare(k, kept, sent, lefts, rights, *outs)


def terms_kernel(a, b, hamiltonian, out):
    for c in range(out.shape[0]):
        for t in range(out.shape[1]):
            inner = multiply((a[c, 0], a[c, 1]), split(hamiltonian[c, t, 0]))
            out[c, t] = multiply(split(inner), (b[c, 0], b[c, 1]))


def finish_kernel(share, passed, rest, terms, norm, out, x):
    rows = share.shape[0]
    at = bit(1).astype(jnp.int32) * rows
    x[pl.ds(pl.multiple_of(at, 8), rows)] = share[...]
    x[pl.ds(pl.multiple_of(rows - at, 8), rows)] = passed[...]
    x[2 * rows :] = rest[...]
    z = product(x[...].T, x[...])
    columns, count = terms.shape[0], terms.shape[1]

    def total(m):
        s = jnp.sum(z * m, axis=0, keepdims=True)
        return sum(s[:, i : i + LANES] for i in range(0, s.shape[1], LANES))

    sums = [total(terms[c, t]) for c in range(columns) for t in range(count)] + [total(norm[...])]
    sums += [jnp.zeros_like(sums[0])] * (out.shape[0] - len(sums))
    out[...] = jnp.concatenate(sums, axis=0)


def left_kernel(k, x, lefts, out):
    @pl.when(bit(k))
    def _():
        xs = split(x[...])
        for c in range(out.shape[0]):
            out[c, 0] = multiply(xs, split(lefts[c]))

    @pl.when(jnp.logical_not(bit(k)))
    def _():
        out[:, 0] = lefts[...]


def energy_kernel(scale, *refs):
    parts, out = [refs[0][...]] + [r[...] for r in refs[-2:0:-1]], refs[-1]
    while len(parts) > 1:
        parts = [a + b for a, b in zip(parts[::2], parts[1::2])]
    columns, terms = out.shape
    s = jnp.sum(parts[0], axis=1, keepdims=True)
    s = jnp.broadcast_to(scale * s / s[columns * terms : columns * terms + 1], parts[0].shape)
    row = lax.broadcasted_iota(jnp.int32, s.shape, 0)
    lane = lax.broadcasted_iota(jnp.int32, s.shape, 1)
    for c in range(columns):
        out[c : c + 1] = jnp.sum(jnp.where(row == c * terms + lane, s, 0.0), axis=0, keepdims=True)[:, :terms]


def call(kernel, outs, flops, *args, smem=0, scratch=()):
    return pl.pallas_call(
        kernel,
        out_shape=outs,
        in_specs=[SMEM] * smem + [VMEM] * (len(args) - smem),
        out_specs=jax.tree.map(lambda _: VMEM, outs),
        scratch_shapes=list(scratch),
        compiler_params=pltpu.CompilerParams(vmem_limit_bytes=LIMIT),
        cost_estimate=pl.CostEstimate(flops=flops, bytes_accessed=1 << 20, transcendentals=0),
    )(*args)


def per_device(transfer, hamiltonian, kept):
    columns, width, terms = transfer.shape[0], transfer.shape[2], hamiltonian.shape[1]
    total, sectors = lax.axis_size("col"), lax.axis_size("sec")
    half = total // 2
    one = 6 * width**3

    def array(*shape, dtype=F32):
        return jax.ShapeDtypeStruct(shape, dtype)

    matrix = array(width, width)
    room = (pltpu.VMEM((width, width), F32),)

    def swap(a, k):
        return lax.ppermute(a, "col", [(i, i ^ k) for i in range(total)])

    heights = [8 * h for h in FIRST]
    n = len(heights)
    own, *parts = call(group_kernel, (matrix,) + tuple(array(h, width) for h in heights), one, transfer)
    nears = [swap(part, 1) for part in parts]
    pairs, fars = [], []
    for near, h in zip(nears, heights):
        pairs.append(call(pair_kernel, array(h, width), one // n, near, own))
        fars.append(swap(pairs[-1], 2))
    both = array(columns, width, width)
    left, right = call(lambda *refs: near_kernel(n, *refs), (both, both), 2 * one, transfer, *nears)
    fars[0], left = lax.optimization_barrier((fars[0], left))
    begun = call(lambda *refs: begin_kernel(n, *refs), matrix, one, *pairs, *fars[:-1])
    rows = 8 * SHARE
    shared = (matrix, array(rows, width), array(width - 2 * rows, width))
    if total <= 8:
        sent, share, rest = call(
            lambda *refs: quad_sent_kernel(n, half, *refs), shared, one, begun, *pairs, fars[-1], scratch=room
        )
    else:
        whole = call(lambda *refs: quad_kernel(n, *refs), matrix, one, begun, *pairs, fars[-1], scratch=room)
        left, right = call(lambda *refs: sides_kernel(n, *refs), (both, both), 2 * one, left, right, *fars)
        k = 4
        while k < half:
            x = swap(whole, k)
            whole, left, right = call(
                lambda *refs, k=k: level_kernel(k, *refs), (matrix, both, both), 5 * one, whole, left, right, x
            )
            k *= 2
        sent, share, rest = call(lambda *refs: sent_kernel(half, *refs), shared, one, whole)
    share = swap(share, half)
    rest = swap(rest, half)
    halves = array(columns, 2, width, width, dtype=BF16)
    prepared = (array(columns, width, width), matrix, halves, halves)
    if total <= 8:
        lefts, norm, a, b = call(
            lambda *refs: prepare_quad_kernel(n, half, *refs), prepared, 5 * one, kept, sent, left, right, *fars,
            scratch=(pltpu.VMEM((columns, width, width), F32),) * 2,
        )
    else:
        lefts, norm, a, b = call(
            lambda *refs: prepare_kernel(half, *refs), prepared, 3 * one, kept, sent, left, right
        )
    share, norm = lax.optimization_barrier((share, norm))
    passed = swap(share, 1)
    products = call(terms_kernel, array(columns, terms, width, width), 12 * one, a, b, hamiltonian)
    table_rows = -(-(columns * terms + 1) // 8) * 8
    table, x = call(
        finish_kernel, (array(table_rows, LANES), matrix), 2 * one, share, passed, rest, products, norm
    )
    parts = [table] + [lax.ppermute(table, "sec", [(i, i ^ k) for i in range(sectors)]) for k in range(sectors - 1, 0, -1)]
    left_env = call(
        lambda *refs: left_kernel(half, *refs), array(columns, 1, width, width), 2 * one, x, lefts
    )
    scale = float(width * sectors)
    energy = call(lambda *refs: energy_kernel(scale, *refs), array(columns, terms), 1000, *parts)
    return left_env, energy


def solution(mesh):
    in_specs = (P("col", "sec", None, None), P("col", None, "sec", None, None), P("col", "sec"))
    out_specs = (P("col", "sec", None, None), P("col", None))
    return jax.shard_map(
        per_device, mesh=mesh, in_specs=in_specs, out_specs=out_specs, check_vma=False
    )
```

```python
import jax
import jax.numpy as jnp
from jax import lax
from jax.experimental import pallas as pl
from jax.experimental.pallas import tpu as pltpu
from jax.sharding import PartitionSpec as P

F32 = jnp.float32
BF16 = jnp.bfloat16
VMEM = pl.BlockSpec(memory_space=pltpu.VMEM)
SMEM = pl.BlockSpec(memory_space=pltpu.SMEM)
LIMIT = 40 * 1024 * 1024
LANES = 128
FIRST = (21, 11)
SHARE = 8


def split(a):
    high = a.astype(BF16)
    return high, (a - high.astype(F32)).astype(BF16)


def dot(a, b, over):
    return lax.dot_general(a, b, (over, ((), ())), preferred_element_type=F32)


def multiply(a, b, over=((1,), (0,))):
    return dot(a[0], b[0], over) + (dot(a[0], b[1], over) + dot(a[1], b[0], over))


def product(a, b):
    return multiply(split(a), split(b))


def bit(k):
    return (lax.axis_index("col") // k) % 2 == 1


def eye(width):
    rows = lax.broadcasted_iota(jnp.int32, (width, width), 0)
    return (rows == lax.broadcasted_iota(jnp.int32, (width, width), 1)).astype(F32)


def group_kernel(transfer, whole, *parts):
    group = product(transfer[0, 0], transfer[1, 0])

    @pl.when(bit(1))
    def _():
        whole[...] = group.T

    @pl.when(jnp.logical_not(bit(1)))
    def _():
        whole[...] = group

    at = 0
    for part in parts:
        part[...] = whole[at : at + part.shape[0]]
        at += part.shape[0]


def pair_kernel(near, own, out):
    out[...] = multiply(split(near[...]), split(own[...]), ((1,), (1,)))


def whole_of(parts):
    return jnp.concatenate([part[...] for part in parts], axis=0)


def begin_kernel(n, *refs):
    pairs, fars, out = refs[:n], refs[n:-1], refs[-1]
    pair, far = whole_of(pairs), whole_of(fars)
    rows = far.shape[0]

    @pl.when(bit(1) == bit(2))
    def _():
        out[:rows] = product(far, pair)
        out[rows:] = jnp.zeros_like(out[rows:])

    @pl.when(bit(1) != bit(2))
    def _():
        out[...] = product(pair[:, :rows], far)


def end_quad(begun, pairs, far, room):
    pair, far = whole_of(pairs), far[...]
    at = pair.shape[0] - far.shape[0]

    @pl.when(bit(1) == bit(2))
    def _():
        room[:at] = begun[:at]
        room[at:] = product(far, pair)

    @pl.when(bit(1) != bit(2))
    def _():
        room[...] = begun[...] + product(pair[:, at:], far)

    return room[...]


def quad_kernel(n, begun, *refs):
    pairs, (far, whole, room) = refs[:n], refs[n:]
    value = end_quad(begun, pairs, far, room)
    whole[...] = jnp.where(bit(1), value, value.T)


def spread(value, flip, sent, share, rest):
    @pl.when(flip)
    def _():
        sent[...] = value.T

    @pl.when(jnp.logical_not(flip))
    def _():
        sent[...] = value

    rows = share.shape[0]
    share[...] = sent[pl.ds(pl.multiple_of(bit(1).astype(jnp.int32) * rows, 8), rows)]
    rest[...] = sent[2 * rows :]


def quad_sent_kernel(n, k, begun, *refs):
    pairs, (far, sent, share, rest, room) = refs[:n], refs[n:]
    spread(end_quad(begun, pairs, far, room), bit(1) == bit(k), sent, share, rest)


def sent_kernel(k, whole, sent, share, rest):
    spread(whole[...], bit(k), sent, share, rest)


def near_kernel(n, transfer, *refs):
    nears, (left, right) = refs[:n], refs[n:]
    odd = bit(1)
    near = whole_of(nears)

    @pl.when(odd)
    def _():
        left[0] = near
        left[1] = product(near, transfer[0, 0])
        right[0] = transfer[1, 0]
        right[1] = eye(near.shape[0])

    @pl.when(jnp.logical_not(odd))
    def _():
        value = near.T
        left[0] = eye(near.shape[0])
        left[1] = transfer[0, 0]
        right[0] = product(transfer[1, 0], value)
        right[1] = value


def sides(left, right, fars, lefts, rights):
    high = bit(2)
    other = whole_of(fars)
    other = split(jnp.where(bit(1), other, other.T))

    @pl.when(high)
    def _():
        rights[...] = right[...]
        for c in range(lefts.shape[0]):
            lefts[c] = multiply(other, split(left[c]))

    @pl.when(jnp.logical_not(high))
    def _():
        lefts[...] = left[...]
        for c in range(lefts.shape[0]):
            rights[c] = multiply(split(right[c]), other)


def sides_kernel(n, left, right, *refs):
    sides(left, right, refs[:n], *refs[n:])


def level_kernel(k, whole, left, right, x, whole_out, left_out, right_out):
    after = bit(k)
    whole, left, right, x = whole[...], left[...], right[...], x[...]
    one = eye(whole.shape[0])
    whole_out[...] = product(jnp.where(after, x, whole), jnp.where(after, whole, x))
    for c in range(left.shape[0]):
        left_out[c] = product(jnp.where(after, x, one), left[c])
        right_out[c] = product(right[c], jnp.where(after, one, x))


def prepare(k, kept, sent, lefts, rights, lefts_out, norm_out, a_out, b_out):
    y, transposed = split(sent[...]), split(sent[...].T)
    norm_out[...] = multiply(transposed, y)
    column = lax.broadcasted_iota(jnp.int32, lefts.shape[1:], 1)
    for c in range(lefts.shape[0]):
        lefts_out[c] = jnp.where(column < kept[c : c + 1], lefts[c], 0.0)

    @pl.when(bit(k))
    def _():
        for c in range(lefts.shape[0]):
            a_out[c, 0], a_out[c, 1] = split(lefts_out[c])
            b_out[c, 0], b_out[c, 1] = split(multiply(split(rights[c]), y))

    @pl.when(jnp.logical_not(bit(k)))
    def _():
        for c in range(lefts.shape[0]):
            a_out[c, 0], a_out[c, 1] = split(multiply(transposed, split(lefts_out[c])))
            b_out[c, 0], b_out[c, 1] = split(rights[c])


def prepare_quad_kernel(n, k, kept, sent, left, right, *refs):
    fars, outs, (lefts, rights) = refs[:n], refs[n:-2], refs[-2:]
    sides(left, right, fars, lefts, rights)
    prepare(k, kept, sent, lefts, rights, *outs)


def prepare_kernel(k, kept, sent, lefts, rights, *outs):
    prepare(k, kept, sent, lefts, rights, *outs)


def terms_kernel(a, b, hamiltonian, out):
    for c in range(out.shape[0]):
        for t in range(out.shape[1]):
            inner = multiply((a[c, 0], a[c, 1]), split(hamiltonian[c, t, 0]))
            out[c, t] = multiply(split(inner), (b[c, 0], b[c, 1]))


def finish_kernel(share, passed, rest, terms, norm, out, x):
    rows = share.shape[0]
    at = bit(1).astype(jnp.int32) * rows
    x[pl.ds(pl.multiple_of(at, 8), rows)] = share[...]
    x[pl.ds(pl.multiple_of(rows - at, 8), rows)] = passed[...]
    x[2 * rows :] = rest[...]
    z = product(x[...].T, x[...])
    columns, count = terms.shape[0], terms.shape[1]

    def total(m):
        s = jnp.sum(z * m, axis=0, keepdims=True)
        return sum(s[:, i : i + LANES] for i in range(0, s.shape[1], LANES))

    sums = [total(terms[c, t]) for c in range(columns) for t in range(count)] + [total(norm[...])]
    sums += [jnp.zeros_like(sums[0])] * (out.shape[0] - len(sums))
    out[...] = jnp.concatenate(sums, axis=0)


def left_kernel(k, x, lefts, out):
    @pl.when(bit(k))
    def _():
        xs = split(x[...])
        for c in range(out.shape[0]):
            out[c, 0] = multiply(xs, split(lefts[c]))

    @pl.when(jnp.logical_not(bit(k)))
    def _():
        out[:, 0] = lefts[...]


def energy_kernel(scale, *refs):
    parts, out = [refs[0][...]] + [r[...] for r in refs[-2:0:-1]], refs[-1]
    while len(parts) > 1:
        parts = [a + b for a, b in zip(parts[::2], parts[1::2])]
    columns, terms = out.shape
    s = jnp.sum(parts[0], axis=1, keepdims=True)
    s = jnp.broadcast_to(scale * s / s[columns * terms : columns * terms + 1], parts[0].shape)
    row = lax.broadcasted_iota(jnp.int32, s.shape, 0)
    lane = lax.broadcasted_iota(jnp.int32, s.shape, 1)
    for c in range(columns):
        out[c : c + 1] = jnp.sum(jnp.where(row == c * terms + lane, s, 0.0), axis=0, keepdims=True)[:, :terms]


def call(kernel, outs, flops, *args, smem=0, scratch=()):
    return pl.pallas_call(
        kernel,
        out_shape=outs,
        in_specs=[SMEM] * smem + [VMEM] * (len(args) - smem),
        out_specs=jax.tree.map(lambda _: VMEM, outs),
        scratch_shapes=list(scratch),
        compiler_params=pltpu.CompilerParams(vmem_limit_bytes=LIMIT),
        cost_estimate=pl.CostEstimate(flops=flops, bytes_accessed=1 << 20, transcendentals=0),
    )(*args)


def per_device(transfer, hamiltonian, kept):
    columns, width, terms = transfer.shape[0], transfer.shape[2], hamiltonian.shape[1]
    total, sectors = lax.axis_size("col"), lax.axis_size("sec")
    half = total // 2
    one = 6 * width**3

    def array(*shape, dtype=F32):
        return jax.ShapeDtypeStruct(shape, dtype)

    matrix = array(width, width)
    room = (pltpu.VMEM((width, width), F32),)

    def swap(a, k):
        return lax.ppermute(a, "col", [(i, i ^ k) for i in range(total)])

    heights = [8 * h for h in FIRST]
    n = len(heights)
    own, *parts = call(group_kernel, (matrix,) + tuple(array(h, width) for h in heights), one, transfer)
    nears = [swap(part, 1) for part in parts]
    pairs, fars = [], []
    for near, h in zip(nears, heights):
        pairs.append(call(pair_kernel, array(h, width), one // n, near, own))
        fars.append(swap(pairs[-1], 2))
    both = array(columns, width, width)
    left, right = call(lambda *refs: near_kernel(n, *refs), (both, both), 2 * one, transfer, *nears)
    fars[0], left = lax.optimization_barrier((fars[0], left))
    begun = call(lambda *refs: begin_kernel(n, *refs), matrix, one, *pairs, *fars[:-1])
    rows = 8 * SHARE
    shared = (matrix, array(rows, width), array(width - 2 * rows, width))
    if total <= 8:
        sent, share, rest = call(
            lambda *refs: quad_sent_kernel(n, half, *refs), shared, one, begun, *pairs, fars[-1], scratch=room
        )
    else:
        whole = call(lambda *refs: quad_kernel(n, *refs), matrix, one, begun, *pairs, fars[-1], scratch=room)
        left, right = call(lambda *refs: sides_kernel(n, *refs), (both, both), 2 * one, left, right, *fars)
        k = 4
        while k < half:
            x = swap(whole, k)
            whole, left, right = call(
                lambda *refs, k=k: level_kernel(k, *refs), (matrix, both, both), 5 * one, whole, left, right, x
            )
            k *= 2
        sent, share, rest = call(lambda *refs: sent_kernel(half, *refs), shared, one, whole)
    share = swap(share, half | 2)
    rest = swap(rest, half)
    halves = array(columns, 2, width, width, dtype=BF16)
    prepared = (array(columns, width, width), matrix, halves, halves)
    if total <= 8:
        lefts, norm, a, b = call(
            lambda *refs: prepare_quad_kernel(n, half, *refs), prepared, 5 * one, kept, sent, left, right, *fars,
            scratch=(pltpu.VMEM((columns, width, width), F32),) * 2,
        )
    else:
        lefts, norm, a, b = call(
            lambda *refs: prepare_kernel(half, *refs), prepared, 3 * one, kept, sent, left, right
        )
    share, norm = lax.optimization_barrier((share, norm))
    passed = swap(share, 1)
    products = call(terms_kernel, array(columns, terms, width, width), 12 * one, a, b, hamiltonian)
    table_rows = -(-(columns * terms + 1) // 8) * 8
    table, x = call(
        finish_kernel, (array(table_rows, LANES), matrix), 2 * one, share, passed, rest, products, norm
    )
    parts = [table] + [lax.ppermute(table, "sec", [(i, i ^ k) for i in range(sectors)]) for k in range(sectors - 1, 0, -1)]
    left_env = call(
        lambda *refs: left_kernel(half, *refs), array(columns, 1, width, width), 2 * one, x, lefts
    )
    scale = float(width * sectors)
    energy = call(lambda *refs: energy_kernel(scale, *refs), array(columns, terms), 1000, *parts)
    return left_env, energy


def solution(mesh):
    in_specs = (P("col", "sec", None, None), P("col", None, "sec", None, None), P("col", "sec"))
    out_specs = (P("col", "sec", None, None), P("col", None))
    return jax.shard_map(
        per_device, mesh=mesh, in_specs=in_specs, out_specs=out_specs, check_vma=False
    )
```

```python
import jax
import jax.numpy as jnp
from jax import lax
from jax.experimental import pallas as pl
from jax.experimental.pallas import tpu as pltpu
from jax.sharding import PartitionSpec as P

F32 = jnp.float32
BF16 = jnp.bfloat16
VMEM = pl.BlockSpec(memory_space=pltpu.VMEM)
LIMIT = 40 * 1024 * 1024
LANES = 128


def split(a):
    high = a.astype(BF16)
    return high, (a - high.astype(F32)).astype(BF16)


def dot(a, b, over):
    return lax.dot_general(a, b, (over, ((), ())), preferred_element_type=F32)


def multiply(a, b, over=((1,), (0,))):
    return dot(a[0], b[0], over) + (dot(a[0], b[1], over) + dot(a[1], b[0], over))


def product(a, b):
    return multiply(split(a), split(b))


def bit(k):
    return (lax.axis_index("col") // k) % 2 == 1


def eye(width):
    rows = lax.broadcasted_iota(jnp.int32, (width, width), 0)
    return (rows == lax.broadcasted_iota(jnp.int32, (width, width), 1)).astype(F32)


def group_kernel(transfer, whole, *parts):
    group = transfer[0, 0]
    for c in range(1, transfer.shape[0]):
        group = product(group, transfer[c, 0])

    @pl.when(bit(1))
    def _():
        whole[...] = group.T

    @pl.when(jnp.logical_not(bit(1)))
    def _():
        whole[...] = group

    at = 0
    for part in parts:
        part[...] = whole[at : at + part.shape[0]]
        at += part.shape[0]


def pair_kernel(near, own, out):
    out[...] = multiply(split(near[...]), split(own[...]), ((1,), (1,)))


def whole_of(parts):
    return jnp.concatenate([part[...] for part in parts], axis=0)


def begin_kernel(n, *refs):
    pairs, fars, out = refs[:n], refs[n:-1], refs[-1]
    pair, far = whole_of(pairs), whole_of(fars)
    rows = far.shape[0]

    @pl.when(bit(1) == bit(2))
    def _():
        out[:rows] = product(far, pair)
        out[rows:] = jnp.zeros_like(out[rows:])

    @pl.when(bit(1) != bit(2))
    def _():
        out[...] = product(pair[:, :rows], far)


def end_quad(begun, pairs, far, room):
    pair, far = whole_of(pairs), far[...]
    at = pair.shape[0] - far.shape[0]

    @pl.when(bit(1) == bit(2))
    def _():
        room[:at] = begun[:at]
        room[at:] = product(far, pair)

    @pl.when(bit(1) != bit(2))
    def _():
        room[...] = begun[...] + product(pair[:, at:], far)

    return room[...]


def quad_kernel(n, begun, *refs):
    pairs, (far, whole, room) = refs[:n], refs[n:]
    value = end_quad(begun, pairs, far, room)
    whole[...] = jnp.where(bit(1), value, value.T)


def spread(value, flip, sent, share, rest):
    @pl.when(flip)
    def _():
        sent[...] = value.T

    @pl.when(jnp.logical_not(flip))
    def _():
        sent[...] = value

    rows = share.shape[0]
    share[...] = sent[pl.ds(pl.multiple_of(bit(1).astype(jnp.int32) * rows, 8), rows)]
    rest[...] = sent[2 * rows :]


def quad_sent_kernel(n, k, begun, *refs):
    pairs, (far, sent, share, rest, room) = refs[:n], refs[n:]
    spread(end_quad(begun, pairs, far, room), bit(1) == bit(k), sent, share, rest)


def sent_kernel(k, whole, sent, share, rest):
    spread(whole[...], bit(k), sent, share, rest)


def near_kernel(n, transfer, *refs):
    nears, (left, right) = refs[:n], refs[n:]
    last = transfer.shape[0] - 1
    near = whole_of(nears)

    @pl.when(bit(1))
    def _():
        left[0] = near
        for c in range(last):
            left[c + 1] = product(left[c], transfer[c, 0])
        right[last] = eye(near.shape[0])
        if last > 0:
            right[last - 1] = transfer[last, 0]
        for c in range(last - 2, -1, -1):
            right[c] = product(transfer[c + 1, 0], right[c + 1])

    @pl.when(jnp.logical_not(bit(1)))
    def _():
        left[0] = eye(near.shape[0])
        if last > 0:
            left[1] = transfer[0, 0]
        for c in range(1, last):
            left[c + 1] = product(left[c], transfer[c, 0])
        right[last] = near.T
        for c in range(last - 1, -1, -1):
            right[c] = product(transfer[c + 1, 0], right[c + 1])


def sides(left, right, fars, lefts, rights):
    high = bit(2)
    other = whole_of(fars)
    other = split(jnp.where(bit(1), other, other.T))

    @pl.when(high)
    def _():
        rights[...] = right[...]
        for c in range(lefts.shape[0]):
            lefts[c] = multiply(other, split(left[c]))

    @pl.when(jnp.logical_not(high))
    def _():
        lefts[...] = left[...]
        for c in range(lefts.shape[0]):
            rights[c] = multiply(split(right[c]), other)


def sides_kernel(n, left, right, *refs):
    sides(left, right, refs[:n], *refs[n:])


def level_kernel(k, whole, left, right, x, whole_out, left_out, right_out):
    after = bit(k)
    whole, left, right, x = whole[...], left[...], right[...], x[...]
    one = eye(whole.shape[0])
    whole_out[...] = product(jnp.where(after, x, whole), jnp.where(after, whole, x))
    for c in range(left.shape[0]):
        left_out[c] = product(jnp.where(after, x, one), left[c])
        right_out[c] = product(right[c], jnp.where(after, one, x))


def prepare(k, kept, sent, lefts, rights, lefts_out, norm_out, a_out, b_out):
    y, transposed = split(sent[...]), split(sent[...].T)
    norm_out[...] = multiply(transposed, y)
    column = lax.broadcasted_iota(jnp.int32, lefts.shape[1:], 1)
    for c in range(lefts.shape[0]):
        lefts_out[c] = jnp.where(column < kept[c : c + 1], lefts[c], 0.0)

    @pl.when(bit(k))
    def _():
        for c in range(lefts.shape[0]):
            a_out[c, 0], a_out[c, 1] = split(lefts_out[c])
            b_out[c, 0], b_out[c, 1] = split(multiply(split(rights[c]), y))

    @pl.when(jnp.logical_not(bit(k)))
    def _():
        for c in range(lefts.shape[0]):
            a_out[c, 0], a_out[c, 1] = split(multiply(transposed, split(lefts_out[c])))
            b_out[c, 0], b_out[c, 1] = split(rights[c])


def prepare_quad_kernel(n, k, kept, sent, left, right, *refs):
    fars, outs, (lefts, rights) = refs[:n], refs[n:-2], refs[-2:]
    sides(left, right, fars, lefts, rights)
    prepare(k, kept, sent, lefts, rights, *outs)


def prepare_kernel(k, kept, sent, lefts, rights, *outs):
    prepare(k, kept, sent, lefts, rights, *outs)


def terms_kernel(a, b, hamiltonian, out):
    for c in range(out.shape[0]):
        for t in range(out.shape[1]):
            inner = multiply((a[c, 0], a[c, 1]), split(hamiltonian[c, t, 0]))
            out[c, t] = multiply(split(inner), (b[c, 0], b[c, 1]))


def finish_kernel(share, passed, rest, terms, norm, out, x):
    rows = share.shape[0]
    at = bit(1).astype(jnp.int32) * rows
    x[pl.ds(pl.multiple_of(at, 8), rows)] = share[...]
    x[pl.ds(pl.multiple_of(rows - at, 8), rows)] = passed[...]
    x[2 * rows :] = rest[...]
    z = product(x[...].T, x[...])
    columns, count = terms.shape[0], terms.shape[1]

    def total(m):
        s = jnp.sum(z * m, axis=0, keepdims=True)
        return sum(s[:, i : i + LANES] for i in range(0, s.shape[1], LANES))

    sums = [total(terms[c, t]) for c in range(columns) for t in range(count)] + [total(norm[...])]
    sums += [jnp.zeros_like(sums[0])] * (out.shape[0] - len(sums))
    out[...] = jnp.concatenate(sums, axis=0)


def left_kernel(k, x, lefts, out):
    @pl.when(bit(k))
    def _():
        xs = split(x[...])
        for c in range(out.shape[0]):
            out[c, 0] = multiply(xs, split(lefts[c]))

    @pl.when(jnp.logical_not(bit(k)))
    def _():
        out[:, 0] = lefts[...]


def energy_kernel(scale, *refs):
    parts, out = [refs[0][...]] + [r[...] for r in refs[-2:0:-1]], refs[-1]
    while len(parts) > 1:
        parts = [a + b for a, b in zip(parts[::2], parts[1::2])]
    columns, terms = out.shape
    s = jnp.sum(parts[0], axis=1, keepdims=True)
    s = jnp.broadcast_to(scale * s / s[columns * terms : columns * terms + 1], parts[0].shape)
    row = lax.broadcasted_iota(jnp.int32, s.shape, 0)
    lane = lax.broadcasted_iota(jnp.int32, s.shape, 1)
    for c in range(columns):
        out[c : c + 1] = jnp.sum(jnp.where(row == c * terms + lane, s, 0.0), axis=0, keepdims=True)[:, :terms]


def call(kernel, outs, flops, *args, scratch=()):
    return pl.pallas_call(
        kernel,
        out_shape=outs,
        in_specs=[VMEM] * len(args),
        out_specs=jax.tree.map(lambda _: VMEM, outs),
        scratch_shapes=list(scratch),
        compiler_params=pltpu.CompilerParams(vmem_limit_bytes=LIMIT),
        cost_estimate=pl.CostEstimate(flops=flops, bytes_accessed=1 << 20, transcendentals=0),
    )(*args)


def per_device(transfer, hamiltonian, kept):
    columns, width, terms = transfer.shape[0], transfer.shape[2], hamiltonian.shape[1]
    total, sectors = lax.axis_size("col"), lax.axis_size("sec")
    half = total // 2
    one = 6 * width**3

    def array(*shape, dtype=F32):
        return jax.ShapeDtypeStruct(shape, dtype)

    matrix = array(width, width)
    room = (pltpu.VMEM((width, width), F32),)

    def swap(a, k):
        return lax.ppermute(a, "col", [(i, i ^ k) for i in range(total)])

    first = width * 21 // 256 * 8
    heights = [first, width - first]
    n = len(heights)
    own, *parts = call(group_kernel, (matrix,) + tuple(array(h, width) for h in heights), one, transfer)
    nears = [swap(part, 1) for part in parts]
    pairs, fars = [], []
    for near, h in zip(nears, heights):
        pairs.append(call(pair_kernel, array(h, width), one // n, near, own))
        fars.append(swap(pairs[-1], 2))
    both = array(columns, width, width)
    left, right = call(lambda *refs: near_kernel(n, *refs), (both, both), 2 * one, transfer, *nears)
    fars[0], left = lax.optimization_barrier((fars[0], left))
    begun = call(lambda *refs: begin_kernel(n, *refs), matrix, one, *pairs, *fars[:-1])
    rows = width // 4
    shared = (matrix, array(rows, width), array(width - 2 * rows, width))
    if total <= 8:
        sent, share, rest = call(
            lambda *refs: quad_sent_kernel(n, half, *refs), shared, one, begun, *pairs, fars[-1], scratch=room
        )
    else:
        whole = call(lambda *refs: quad_kernel(n, *refs), matrix, one, begun, *pairs, fars[-1], scratch=room)
        left, right = call(lambda *refs: sides_kernel(n, *refs), (both, both), 2 * one, left, right, *fars)
        k = 4
        while k < half:
            x = swap(whole, k)
            whole, left, right = call(
                lambda *refs, k=k: level_kernel(k, *refs), (matrix, both, both), 5 * one, whole, left, right, x
            )
            k *= 2
        sent, share, rest = call(lambda *refs: sent_kernel(half, *refs), shared, one, whole)
    share = swap(share, half | 2)
    rest = swap(rest, half)
    halves = array(columns, 2, width, width, dtype=BF16)
    prepared = (array(columns, width, width), matrix, halves, halves)
    if total <= 8:
        lefts, norm, a, b = call(
            lambda *refs: prepare_quad_kernel(n, half, *refs), prepared, 5 * one, kept, sent, left, right, *fars,
            scratch=(pltpu.VMEM((columns, width, width), F32),) * 2,
        )
    else:
        lefts, norm, a, b = call(
            lambda *refs: prepare_kernel(half, *refs), prepared, 3 * one, kept, sent, left, right
        )
    share, norm = lax.optimization_barrier((share, norm))
    passed = swap(share, 1)
    products = call(terms_kernel, array(columns, terms, width, width), 12 * one, a, b, hamiltonian)
    table_rows = -(-(columns * terms + 1) // 8) * 8
    table, x = call(
        finish_kernel, (array(table_rows, LANES), matrix), 2 * one, share, passed, rest, products, norm
    )
    parts = [table] + [lax.ppermute(table, "sec", [(i, i ^ k) for i in range(sectors)]) for k in range(sectors - 1, 0, -1)]
    left_env = call(
        lambda *refs: left_kernel(half, *refs), array(columns, 1, width, width), 2 * one, x, lefts
    )
    scale = float(width * sectors)
    energy = call(lambda *refs: energy_kernel(scale, *refs), array(columns, terms), 1000, *parts)
    return left_env, energy


def solution(mesh):
    in_specs = (P("col", "sec", None, None), P("col", None, "sec", None, None), P("col", "sec"))
    out_specs = (P("col", "sec", None, None), P("col", None))
    return jax.shard_map(
        per_device, mesh=mesh, in_specs=in_specs, out_specs=out_specs, check_vma=False
    )
```

```python
import jax
import jax.numpy as jnp
from jax import lax
from jax.experimental import pallas as pl
from jax.experimental.pallas import tpu as pltpu
from jax.sharding import PartitionSpec as P

F32 = jnp.float32
BF16 = jnp.bfloat16
VMEM = pl.BlockSpec(memory_space=pltpu.VMEM)
LIMIT = 40 * 1024 * 1024
LANES = 128


def split(a):
    high = a.astype(BF16)
    return high, (a - high.astype(F32)).astype(BF16)


def dot(a, b, over):
    return lax.dot_general(a, b, (over, ((), ())), preferred_element_type=F32)


def multiply(a, b, over=((1,), (0,))):
    return dot(a[0], b[0], over) + (dot(a[0], b[1], over) + dot(a[1], b[0], over))


def product(a, b):
    return multiply(split(a), split(b))


def bit(k):
    return (lax.axis_index("col") // k) % 2 == 1


def eye(width):
    rows = lax.broadcasted_iota(jnp.int32, (width, width), 0)
    return (rows == lax.broadcasted_iota(jnp.int32, (width, width), 1)).astype(F32)


def group_kernel(transfer, whole, *parts):
    group = transfer[0, 0]
    for c in range(1, transfer.shape[0]):
        group = product(group, transfer[c, 0])

    @pl.when(bit(1))
    def _():
        whole[...] = group.T

    @pl.when(jnp.logical_not(bit(1)))
    def _():
        whole[...] = group

    at = 0
    for part in parts:
        part[...] = whole[at : at + part.shape[0]]
        at += part.shape[0]


def turn_kernel(whole, turned):
    turned[0], turned[1] = split(whole[...].T)


def pair_kernel(near, turned, out):
    out[...] = multiply(split(near[...]), (turned[0], turned[1]))


def whole_of(parts):
    return jnp.concatenate([part[...] for part in parts], axis=0)


def begin_kernel(n, *refs):
    pairs, fars, out = refs[:n], refs[n:-1], refs[-1]
    pair, far = whole_of(pairs), whole_of(fars)
    rows = far.shape[0]

    @pl.when(bit(1) == bit(2))
    def _():
        out[:rows] = product(far, pair)
        out[rows:] = jnp.zeros_like(out[rows:])

    @pl.when(bit(1) != bit(2))
    def _():
        out[...] = product(pair[:, :rows], far)


def end_quad(begun, pairs, far, room):
    pair, far = whole_of(pairs), far[...]
    at = pair.shape[0] - far.shape[0]

    @pl.when(bit(1) == bit(2))
    def _():
        room[:at] = begun[:at]
        room[at:] = product(far, pair)

    @pl.when(bit(1) != bit(2))
    def _():
        room[...] = begun[...] + product(pair[:, at:], far)

    return room[...]


def quad_kernel(n, begun, *refs):
    pairs, (far, whole, room) = refs[:n], refs[n:]
    value = end_quad(begun, pairs, far, room)
    whole[...] = jnp.where(bit(1), value, value.T)


def spread(value, flip, sent, share, rest):
    @pl.when(flip)
    def _():
        sent[...] = value.T

    @pl.when(jnp.logical_not(flip))
    def _():
        sent[...] = value

    rows = share.shape[0]
    share[...] = sent[pl.ds(pl.multiple_of(bit(1).astype(jnp.int32) * rows, 8), rows)]
    rest[...] = sent[2 * rows :]


def quad_sent_kernel(n, k, begun, *refs):
    pairs, (far, sent, share, rest, room) = refs[:n], refs[n:]
    spread(end_quad(begun, pairs, far, room), bit(1) == bit(k), sent, share, rest)


def sent_kernel(k, whole, sent, share, rest):
    spread(whole[...], bit(k), sent, share, rest)


def near_kernel(n, kept, transfer, *refs):
    nears, (left, right) = refs[:n], refs[n:]
    last = transfer.shape[0] - 1
    near = whole_of(nears)

    @pl.when(bit(1))
    def _():
        left[0] = near
        for c in range(last):
            left[c + 1] = product(left[c], transfer[c, 0])
        right[last] = eye(near.shape[0])
        if last > 0:
            right[last - 1] = transfer[last, 0]
        for c in range(last - 2, -1, -1):
            right[c] = product(transfer[c + 1, 0], right[c + 1])

    @pl.when(jnp.logical_not(bit(1)))
    def _():
        left[0] = eye(near.shape[0])
        if last > 0:
            left[1] = transfer[0, 0]
        for c in range(1, last):
            left[c + 1] = product(left[c], transfer[c, 0])
        right[last] = near.T
        for c in range(last - 1, -1, -1):
            right[c] = product(transfer[c + 1, 0], right[c + 1])

    column = lax.broadcasted_iota(jnp.int32, near.shape, 1)
    for c in range(last + 1):
        left[c] = jnp.where(column < kept[c : c + 1], left[c], 0.0)


def sides(left, right, fars, lefts, rights):
    high = bit(2)
    other = whole_of(fars)
    other = split(jnp.where(bit(1), other, other.T))

    @pl.when(high)
    def _():
        rights[...] = right[...]
        for c in range(lefts.shape[0]):
            lefts[c] = multiply(other, split(left[c]))

    @pl.when(jnp.logical_not(high))
    def _():
        lefts[...] = left[...]
        for c in range(lefts.shape[0]):
            rights[c] = multiply(split(right[c]), other)


def sides_kernel(n, left, right, *refs):
    sides(left, right, refs[:n], *refs[n:])


def level_kernel(k, whole, left, right, x, whole_out, left_out, right_out):
    after = bit(k)
    whole, left, right, x = whole[...], left[...], right[...], x[...]
    one = eye(whole.shape[0])
    whole_out[...] = product(jnp.where(after, x, whole), jnp.where(after, whole, x))
    for c in range(left.shape[0]):
        left_out[c] = product(jnp.where(after, x, one), left[c])
        right_out[c] = product(right[c], jnp.where(after, one, x))


def prepare(k, sent, lefts, rights, norm_out, a_out, b_out):
    y, transposed = split(sent[...]), split(sent[...].T)
    norm_out[...] = multiply(transposed, y)

    @pl.when(bit(k))
    def _():
        for c in range(lefts.shape[0]):
            a_out[c, 0], a_out[c, 1] = split(lefts[c])
            b_out[c, 0], b_out[c, 1] = split(multiply(split(rights[c]), y))

    @pl.when(jnp.logical_not(bit(k)))
    def _():
        for c in range(lefts.shape[0]):
            a_out[c, 0], a_out[c, 1] = split(multiply(transposed, split(lefts[c])))
            b_out[c, 0], b_out[c, 1] = split(rights[c])


def prepare_quad_kernel(n, k, sent, left, right, *refs):
    fars, (lefts, *outs), rights = refs[:n], refs[n:-1], refs[-1]
    sides(left, right, fars, lefts, rights)
    prepare(k, sent, lefts, rights, *outs)


def prepare_kernel(k, sent, left, right, lefts, *outs):
    lefts[...] = left[...]
    prepare(k, sent, lefts, right, *outs)


def terms_kernel(a, b, hamiltonian, out):
    for c in range(out.shape[0]):
        for t in range(out.shape[1]):
            inner = multiply((a[c, 0], a[c, 1]), split(hamiltonian[c, t, 0]))
            out[c, t] = multiply(split(inner), (b[c, 0], b[c, 1]))


def finish_kernel(share, passed, rest, terms, norm, out, x):
    rows = share.shape[0]
    at = bit(1).astype(jnp.int32) * rows
    x[pl.ds(pl.multiple_of(at, 8), rows)] = share[...]
    x[pl.ds(pl.multiple_of(rows - at, 8), rows)] = passed[...]
    x[2 * rows :] = rest[...]
    z = product(x[...].T, x[...])
    columns, count = terms.shape[0], terms.shape[1]

    def total(m):
        s = jnp.sum(z * m, axis=0, keepdims=True)
        return sum(s[:, i : i + LANES] for i in range(0, s.shape[1], LANES))

    sums = [total(terms[c, t]) for c in range(columns) for t in range(count)] + [total(norm[...])]
    sums += [jnp.zeros_like(sums[0])] * (out.shape[0] - len(sums))
    out[...] = jnp.concatenate(sums, axis=0)


def left_kernel(k, x, lefts, out):
    @pl.when(bit(k))
    def _():
        xs = split(x[...])
        for c in range(out.shape[0]):
            out[c, 0] = multiply(xs, split(lefts[c]))

    @pl.when(jnp.logical_not(bit(k)))
    def _():
        out[:, 0] = lefts[...]


def energy_kernel(scale, *refs):
    parts, out = [refs[0][...]] + [r[...] for r in refs[-2:0:-1]], refs[-1]
    while len(parts) > 1:
        parts = [a + b for a, b in zip(parts[::2], parts[1::2])]
    columns, terms = out.shape
    s = jnp.sum(parts[0], axis=1, keepdims=True)
    s = jnp.broadcast_to(scale * s / s[columns * terms : columns * terms + 1], parts[0].shape)
    row = lax.broadcasted_iota(jnp.int32, s.shape, 0)
    lane = lax.broadcasted_iota(jnp.int32, s.shape, 1)
    for c in range(columns):
        out[c : c + 1] = jnp.sum(jnp.where(row == c * terms + lane, s, 0.0), axis=0, keepdims=True)[:, :terms]


def call(kernel, outs, flops, *args, scratch=()):
    return pl.pallas_call(
        kernel,
        out_shape=outs,
        in_specs=[VMEM] * len(args),
        out_specs=jax.tree.map(lambda _: VMEM, outs),
        scratch_shapes=list(scratch),
        compiler_params=pltpu.CompilerParams(vmem_limit_bytes=LIMIT),
        cost_estimate=pl.CostEstimate(flops=flops, bytes_accessed=1 << 20, transcendentals=0),
    )(*args)


def per_device(transfer, hamiltonian, kept):
    columns, width, terms = transfer.shape[0], transfer.shape[2], hamiltonian.shape[1]
    total, sectors = lax.axis_size("col"), lax.axis_size("sec")
    half = total // 2
    one = 6 * width**3

    def array(*shape, dtype=F32):
        return jax.ShapeDtypeStruct(shape, dtype)

    matrix = array(width, width)
    room = (pltpu.VMEM((width, width), F32),)

    def swap(a, k):
        return lax.ppermute(a, "col", [(i, i ^ k) for i in range(total)])

    first = width * 21 // 256 * 8
    heights = [first, width - first]
    n = len(heights)
    whole, *parts = call(group_kernel, (matrix,) + tuple(array(h, width) for h in heights), one, transfer)
    turned = call(turn_kernel, array(2, width, width, dtype=BF16), one // 4, whole)
    nears = [swap(part, 1) for part in parts]
    pairs, fars = [], []
    for near, h in zip(nears, heights):
        pairs.append(call(pair_kernel, array(h, width), one // n, near, turned))
        fars.append(swap(pairs[-1], 2))
    both = array(columns, width, width)
    left, right = call(lambda *refs: near_kernel(n, *refs), (both, both), 2 * one, kept, transfer, *nears)
    fars[0], left = lax.optimization_barrier((fars[0], left))
    begun = call(lambda *refs: begin_kernel(n, *refs), matrix, one, *pairs, *fars[:-1])
    rows = width // 4
    shared = (matrix, array(rows, width), array(width - 2 * rows, width))
    if total <= 8:
        sent, share, rest = call(
            lambda *refs: quad_sent_kernel(n, half, *refs), shared, one, begun, *pairs, fars[-1], scratch=room
        )
    else:
        whole = call(lambda *refs: quad_kernel(n, *refs), matrix, one, begun, *pairs, fars[-1], scratch=room)
        left, right = call(lambda *refs: sides_kernel(n, *refs), (both, both), 2 * one, left, right, *fars)
        k = 4
        while k < half:
            x = swap(whole, k)
            whole, left, right = call(
                lambda *refs, k=k: level_kernel(k, *refs), (matrix, both, both), 5 * one, whole, left, right, x
            )
            k *= 2
        sent, share, rest = call(lambda *refs: sent_kernel(half, *refs), shared, one, whole)
    share = swap(share, half | 2)
    rest = swap(rest, half)
    halves = array(columns, 2, width, width, dtype=BF16)
    prepared = (array(columns, width, width), matrix, halves, halves)
    if total <= 8:
        lefts, norm, a, b = call(
            lambda *refs: prepare_quad_kernel(n, half, *refs), prepared, 5 * one, sent, left, right, *fars,
            scratch=(pltpu.VMEM((columns, width, width), F32),),
        )
    else:
        lefts, norm, a, b = call(
            lambda *refs: prepare_kernel(half, *refs), prepared, 3 * one, sent, left, right
        )
    share, norm = lax.optimization_barrier((share, norm))
    passed = swap(share, 1)
    products = call(terms_kernel, array(columns, terms, width, width), 12 * one, a, b, hamiltonian)
    table_rows = -(-(columns * terms + 1) // 8) * 8
    table, x = call(
        finish_kernel, (array(table_rows, LANES), matrix), 2 * one, share, passed, rest, products, norm
    )
    parts = [table] + [lax.ppermute(table, "sec", [(i, i ^ k) for i in range(sectors)]) for k in range(sectors - 1, 0, -1)]
    left_env = call(
        lambda *refs: left_kernel(half, *refs), array(columns, 1, width, width), 2 * one, x, lefts
    )
    scale = float(width * sectors)
    energy = call(lambda *refs: energy_kernel(scale, *refs), array(columns, terms), 1000, *parts)
    return left_env, energy


def solution(mesh):
    in_specs = (P("col", "sec", None, None), P("col", None, "sec", None, None), P("col", "sec"))
    out_specs = (P("col", "sec", None, None), P("col", None))
    return jax.shard_map(
        per_device, mesh=mesh, in_specs=in_specs, out_specs=out_specs, check_vma=False
    )
```

```python
import jax
import jax.numpy as jnp
from jax import lax
from jax.experimental import pallas as pl
from jax.experimental.pallas import tpu as pltpu
from jax.sharding import PartitionSpec as P

F32 = jnp.float32
BF16 = jnp.bfloat16
VMEM = pl.BlockSpec(memory_space=pltpu.VMEM)
LIMIT = 40 * 1024 * 1024
LANES = 128


def split(a):
    high = a.astype(BF16)
    return high, (a - high.astype(F32)).astype(BF16)


def dot(a, b, over):
    return lax.dot_general(a, b, (over, ((), ())), preferred_element_type=F32)


def multiply(a, b, over=((1,), (0,))):
    return dot(a[0], b[0], over) + (dot(a[0], b[1], over) + dot(a[1], b[0], over))


def product(a, b):
    return multiply(split(a), split(b))


def bit(k):
    return (lax.axis_index("col") // k) % 2 == 1


def eye(width):
    rows = lax.broadcasted_iota(jnp.int32, (width, width), 0)
    return (rows == lax.broadcasted_iota(jnp.int32, (width, width), 1)).astype(F32)


def group_kernel(transfer, whole, *parts):
    group = transfer[0, 0]
    for c in range(1, transfer.shape[0]):
        group = product(group, transfer[c, 0])

    @pl.when(bit(1))
    def _():
        whole[...] = group.T

    @pl.when(jnp.logical_not(bit(1)))
    def _():
        whole[...] = group

    at = 0
    for part in parts:
        part[...] = whole[at : at + part.shape[0]]
        at += part.shape[0]


def turn_kernel(whole, turned):
    turned[0], turned[1] = split(whole[...].T)


def pair_kernel(near, turned, out):
    out[...] = multiply(split(near[...]), (turned[0], turned[1]))


def whole_of(parts):
    return jnp.concatenate([part[...] for part in parts], axis=0)


def begin_kernel(n, *refs):
    pairs, fars, out = refs[:n], refs[n:-1], refs[-1]
    pair, far = whole_of(pairs), whole_of(fars)
    rows = far.shape[0]

    @pl.when(bit(1) == bit(2))
    def _():
        out[:rows] = product(far, pair)
        out[rows:] = jnp.zeros_like(out[rows:])

    @pl.when(bit(1) != bit(2))
    def _():
        out[...] = product(pair[:, :rows], far)


def end_quad(begun, pairs, far, room):
    pair, far = whole_of(pairs), far[...]
    at = pair.shape[0] - far.shape[0]

    @pl.when(bit(1) == bit(2))
    def _():
        room[:at] = begun[:at]
        room[at:] = product(far, pair)

    @pl.when(bit(1) != bit(2))
    def _():
        room[...] = begun[...] + product(pair[:, at:], far)

    return room[...]


def quad_kernel(n, begun, *refs):
    pairs, (far, whole, room) = refs[:n], refs[n:]
    value = end_quad(begun, pairs, far, room)
    whole[...] = jnp.where(bit(1), value, value.T)


def spread(value, flip, sent, share, rest):
    @pl.when(flip)
    def _():
        sent[...] = value.T

    @pl.when(jnp.logical_not(flip))
    def _():
        sent[...] = value

    rows = share.shape[0]
    share[...] = sent[pl.ds(pl.multiple_of(bit(1).astype(jnp.int32) * rows, 8), rows)]
    rest[...] = sent[2 * rows :]


def quad_sent_kernel(n, k, begun, *refs):
    pairs, (far, sent, share, rest, room) = refs[:n], refs[n:]
    spread(end_quad(begun, pairs, far, room), bit(1) == bit(k), sent, share, rest)


def sent_kernel(k, whole, sent, share, rest):
    spread(whole[...], bit(k), sent, share, rest)


def near_kernel(n, kept, transfer, *refs):
    nears, (left, right) = refs[:n], refs[n:]
    last = transfer.shape[0] - 1
    near = whole_of(nears)

    @pl.when(bit(1))
    def _():
        left[0] = near
        for c in range(last):
            left[c + 1] = product(left[c], transfer[c, 0])
        right[last] = eye(near.shape[0])
        if last > 0:
            right[last - 1] = transfer[last, 0]
        for c in range(last - 2, -1, -1):
            right[c] = product(transfer[c + 1, 0], right[c + 1])

    @pl.when(jnp.logical_not(bit(1)))
    def _():
        left[0] = eye(near.shape[0])
        if last > 0:
            left[1] = transfer[0, 0]
        for c in range(1, last):
            left[c + 1] = product(left[c], transfer[c, 0])
        right[last] = near.T
        for c in range(last - 1, -1, -1):
            right[c] = product(transfer[c + 1, 0], right[c + 1])

    column = lax.broadcasted_iota(jnp.int32, near.shape, 1)
    for c in range(last + 1):
        left[c] = jnp.where(column < kept[c : c + 1], left[c], 0.0)


def sides(left, right, fars, lefts, rights):
    high = bit(2)
    other = whole_of(fars)
    other = split(jnp.where(bit(1), other, other.T))

    @pl.when(high)
    def _():
        rights[...] = right[...]
        for c in range(lefts.shape[0]):
            lefts[c] = multiply(other, split(left[c]))

    @pl.when(jnp.logical_not(high))
    def _():
        lefts[...] = left[...]
        for c in range(lefts.shape[0]):
            rights[c] = multiply(split(right[c]), other)


def sides_kernel(n, left, right, *refs):
    sides(left, right, refs[:n], *refs[n:])


def level_kernel(k, whole, left, right, x, whole_out, left_out, right_out):
    after = bit(k)
    whole, left, right, x = whole[...], left[...], right[...], x[...]
    one = eye(whole.shape[0])
    whole_out[...] = product(jnp.where(after, x, whole), jnp.where(after, whole, x))
    for c in range(left.shape[0]):
        left_out[c] = product(jnp.where(after, x, one), left[c])
        right_out[c] = product(right[c], jnp.where(after, one, x))


def prepare(k, sent, lefts, rights, norm_out, a_out, b_out):
    y, transposed = split(sent[...]), split(sent[...].T)
    norm_out[...] = multiply(transposed, y)

    @pl.when(bit(k))
    def _():
        for c in range(lefts.shape[0]):
            a_out[c, 0], a_out[c, 1] = split(lefts[c])
            b_out[c, 0], b_out[c, 1] = split(multiply(split(rights[c]), y))

    @pl.when(jnp.logical_not(bit(k)))
    def _():
        for c in range(lefts.shape[0]):
            a_out[c, 0], a_out[c, 1] = split(multiply(transposed, split(lefts[c])))
            b_out[c, 0], b_out[c, 1] = split(rights[c])


def prepare_quad_kernel(n, k, sent, left, right, *refs):
    fars, (lefts, *outs), rights = refs[:n], refs[n:-1], refs[-1]
    sides(left, right, fars, lefts, rights)
    prepare(k, sent, lefts, rights, *outs)


def prepare_kernel(k, sent, left, right, lefts, *outs):
    lefts[...] = left[...]
    prepare(k, sent, lefts, right, *outs)


def terms_kernel(a, b, hamiltonian, out):
    for c in range(out.shape[0]):
        for t in range(out.shape[1]):
            inner = multiply((a[c, 0], a[c, 1]), split(hamiltonian[c, t, 0]))
            out[c, t] = multiply(split(inner), (b[c, 0], b[c, 1]))


def finish_kernel(share, passed, rest, terms, norm, out, x):
    rows = share.shape[0]
    at = bit(1).astype(jnp.int32) * rows
    x[pl.ds(pl.multiple_of(at, 8), rows)] = share[...]
    x[pl.ds(pl.multiple_of(rows - at, 8), rows)] = passed[...]
    x[2 * rows :] = rest[...]
    z = product(x[...].T, x[...])
    columns, count = terms.shape[0], terms.shape[1]

    def total(m):
        s = jnp.sum(z * m, axis=0, keepdims=True)
        return sum(s[:, i : i + LANES] for i in range(0, s.shape[1], LANES))

    sums = [total(terms[c, t]) for c in range(columns) for t in range(count)] + [total(norm[...])]
    sums += [jnp.zeros_like(sums[0])] * (out.shape[0] - len(sums))
    out[...] = jnp.concatenate(sums, axis=0)


def left_kernel(k, x, lefts, out):
    @pl.when(bit(k))
    def _():
        xs = split(x[...])
        for c in range(out.shape[0]):
            out[c, 0] = multiply(xs, split(lefts[c]))

    @pl.when(jnp.logical_not(bit(k)))
    def _():
        out[:, 0] = lefts[...]


def energy_kernel(scale, *refs):
    parts, out = [refs[0][...]] + [r[...] for r in refs[-2:0:-1]], refs[-1]
    while len(parts) > 1:
        parts = [a + b for a, b in zip(parts[::2], parts[1::2])]
    columns, terms = out.shape
    s = jnp.sum(parts[0], axis=1, keepdims=True)
    s = jnp.broadcast_to(scale * s / s[columns * terms : columns * terms + 1], parts[0].shape)
    row = lax.broadcasted_iota(jnp.int32, s.shape, 0)
    lane = lax.broadcasted_iota(jnp.int32, s.shape, 1)
    for c in range(columns):
        out[c : c + 1] = jnp.sum(jnp.where(row == c * terms + lane, s, 0.0), axis=0, keepdims=True)[:, :terms]


def call(kernel, outs, flops, *args, scratch=()):
    return pl.pallas_call(
        kernel,
        out_shape=outs,
        in_specs=[VMEM] * len(args),
        out_specs=jax.tree.map(lambda _: VMEM, outs),
        scratch_shapes=list(scratch),
        compiler_params=pltpu.CompilerParams(vmem_limit_bytes=LIMIT),
        cost_estimate=pl.CostEstimate(flops=flops, bytes_accessed=1 << 20, transcendentals=0),
    )(*args)


def per_device(transfer, hamiltonian, kept):
    columns, width, terms = transfer.shape[0], transfer.shape[2], hamiltonian.shape[1]
    total, sectors = lax.axis_size("col"), lax.axis_size("sec")
    half = total // 2
    one = 6 * width**3

    def array(*shape, dtype=F32):
        return jax.ShapeDtypeStruct(shape, dtype)

    matrix = array(width, width)
    room = (pltpu.VMEM((width, width), F32),)

    def swap(a, k):
        return lax.ppermute(a, "col", [(i, i ^ k) for i in range(total)])

    first = width * 21 // 256 * 8
    heights = [first, width - first]
    n = len(heights)
    whole, *parts = call(group_kernel, (matrix,) + tuple(array(h, width) for h in heights), one, transfer)
    turned = call(turn_kernel, array(2, width, width, dtype=BF16), one // 4, whole)
    nears = [swap(part, 1) for part in parts]
    pairs, fars = [], []
    for near, h in zip(nears, heights):
        pairs.append(call(pair_kernel, array(h, width), one // n, near, turned))
        fars.append(swap(pairs[-1], 2))
    both = array(columns, width, width)
    left, right = call(lambda *refs: near_kernel(n, *refs), (both, both), 2 * one, kept, transfer, *nears)
    fars[0], left = lax.optimization_barrier((fars[0], left))
    begun = call(lambda *refs: begin_kernel(n, *refs), matrix, one, *pairs, *fars[:-1])
    rows = width * 7 // 256 * 8
    shared = (matrix, array(rows, width), array(width - 2 * rows, width))
    if total <= 8:
        sent, share, rest = call(
            lambda *refs: quad_sent_kernel(n, half, *refs), shared, one, begun, *pairs, fars[-1], scratch=room
        )
    else:
        whole = call(lambda *refs: quad_kernel(n, *refs), matrix, one, begun, *pairs, fars[-1], scratch=room)
        left, right = call(lambda *refs: sides_kernel(n, *refs), (both, both), 2 * one, left, right, *fars)
        k = 4
        while k < half:
            x = swap(whole, k)
            whole, left, right = call(
                lambda *refs, k=k: level_kernel(k, *refs), (matrix, both, both), 5 * one, whole, left, right, x
            )
            k *= 2
        sent, share, rest = call(lambda *refs: sent_kernel(half, *refs), shared, one, whole)
    share = swap(share, half | 2)
    rest = swap(rest, half)
    halves = array(columns, 2, width, width, dtype=BF16)
    prepared = (array(columns, width, width), matrix, halves, halves)
    if total <= 8:
        lefts, norm, a, b = call(
            lambda *refs: prepare_quad_kernel(n, half, *refs), prepared, 5 * one, sent, left, right, *fars,
            scratch=(pltpu.VMEM((columns, width, width), F32),),
        )
    else:
        lefts, norm, a, b = call(
            lambda *refs: prepare_kernel(half, *refs), prepared, 3 * one, sent, left, right
        )
    share, norm = lax.optimization_barrier((share, norm))
    passed = swap(share, 1)
    products = call(terms_kernel, array(columns, terms, width, width), 12 * one, a, b, hamiltonian)
    table_rows = -(-(columns * terms + 1) // 8) * 8
    table, x = call(
        finish_kernel, (array(table_rows, LANES), matrix), 2 * one, share, passed, rest, products, norm
    )
    parts = [table] + [lax.ppermute(table, "sec", [(i, i ^ k) for i in range(sectors)]) for k in range(sectors - 1, 0, -1)]
    left_env = call(
        lambda *refs: left_kernel(half, *refs), array(columns, 1, width, width), 2 * one, x, lefts
    )
    scale = float(width * sectors)
    energy = call(lambda *refs: energy_kernel(scale, *refs), array(columns, terms), 1000, *parts)
    return left_env, energy


def solution(mesh):
    in_specs = (P("col", "sec", None, None), P("col", None, "sec", None, None), P("col", "sec"))
    out_specs = (P("col", "sec", None, None), P("col", None))
    return jax.shard_map(
        per_device, mesh=mesh, in_specs=in_specs, out_specs=out_specs, check_vma=False
    )
```

```python
import jax
import jax.numpy as jnp
from jax import lax
from jax.experimental import pallas as pl
from jax.experimental.pallas import tpu as pltpu
from jax.sharding import PartitionSpec as P

F32 = jnp.float32
BF16 = jnp.bfloat16
VMEM = pl.BlockSpec(memory_space=pltpu.VMEM)
LIMIT = 40 * 1024 * 1024
LANES = 128


def split(a):
    high = a.astype(BF16)
    return high, (a - high.astype(F32)).astype(BF16)


def dot(a, b, over):
    return lax.dot_general(a, b, (over, ((), ())), preferred_element_type=F32)


def multiply(a, b, over=((1,), (0,))):
    return dot(a[0], b[0], over) + (dot(a[0], b[1], over) + dot(a[1], b[0], over))


def product(a, b):
    return multiply(split(a), split(b))


def bit(k):
    return (lax.axis_index("col") // k) % 2 == 1


def eye(width):
    rows = lax.broadcasted_iota(jnp.int32, (width, width), 0)
    return (rows == lax.broadcasted_iota(jnp.int32, (width, width), 1)).astype(F32)


def group_kernel(transfer, whole, *parts):
    group = transfer[0, 0]
    for c in range(1, transfer.shape[0]):
        group = product(group, transfer[c, 0])

    @pl.when(bit(1))
    def _():
        whole[...] = group.T

    @pl.when(jnp.logical_not(bit(1)))
    def _():
        whole[...] = group

    at = 0
    for part in parts:
        part[...] = whole[at : at + part.shape[0]]
        at += part.shape[0]


def turn_kernel(whole, turned):
    turned[0], turned[1] = split(whole[...].T)


def pair_kernel(near, turned, out):
    out[...] = multiply(split(near[...]), (turned[0], turned[1]))


def whole_of(parts):
    return jnp.concatenate([part[...] for part in parts], axis=0)


def begin_kernel(n, *refs):
    pairs, fars, out = refs[:n], refs[n:-1], refs[-1]
    pair, far = whole_of(pairs), whole_of(fars)
    rows = far.shape[0]

    @pl.when(bit(1) == bit(2))
    def _():
        out[:rows] = product(far, pair)
        out[rows:] = jnp.zeros_like(out[rows:])

    @pl.when(bit(1) != bit(2))
    def _():
        out[...] = product(pair[:, :rows], far)


def end_quad(begun, pairs, far, room):
    pair, far = whole_of(pairs), far[...]
    at = pair.shape[0] - far.shape[0]

    @pl.when(bit(1) == bit(2))
    def _():
        room[:at] = begun[:at]
        room[at:] = product(far, pair)

    @pl.when(bit(1) != bit(2))
    def _():
        room[...] = begun[...] + product(pair[:, at:], far)

    return room[...]


def quad_kernel(n, begun, *refs):
    pairs, (far, whole, room) = refs[:n], refs[n:]
    value = end_quad(begun, pairs, far, room)
    whole[...] = jnp.where(bit(1), value, value.T)


def spread(value, flip, sent, share, rest):
    @pl.when(flip)
    def _():
        sent[...] = value.T

    @pl.when(jnp.logical_not(flip))
    def _():
        sent[...] = value

    rows = share.shape[0]
    share[...] = sent[pl.ds(pl.multiple_of(bit(1).astype(jnp.int32) * rows, 8), rows)]
    rest[...] = sent[2 * rows :]


def quad_sent_kernel(n, k, begun, *refs):
    pairs, (far, sent, share, rest, room) = refs[:n], refs[n:]
    spread(end_quad(begun, pairs, far, room), bit(1) == bit(k), sent, share, rest)


def sent_kernel(k, whole, sent, share, rest):
    spread(whole[...], bit(k), sent, share, rest)


def near_kernel(n, kept, transfer, *refs):
    nears, (left, right) = refs[:n], refs[n:]
    last = transfer.shape[0] - 1
    near = whole_of(nears)

    @pl.when(bit(1))
    def _():
        left[0] = near
        for c in range(last):
            left[c + 1] = product(left[c], transfer[c, 0])
        right[last] = eye(near.shape[0])
        if last > 0:
            right[last - 1] = transfer[last, 0]
        for c in range(last - 2, -1, -1):
            right[c] = product(transfer[c + 1, 0], right[c + 1])

    @pl.when(jnp.logical_not(bit(1)))
    def _():
        left[0] = eye(near.shape[0])
        if last > 0:
            left[1] = transfer[0, 0]
        for c in range(1, last):
            left[c + 1] = product(left[c], transfer[c, 0])
        right[last] = near.T
        for c in range(last - 1, -1, -1):
            right[c] = product(transfer[c + 1, 0], right[c + 1])

    column = lax.broadcasted_iota(jnp.int32, near.shape, 1)
    for c in range(last + 1):
        left[c] = jnp.where(column < kept[c : c + 1], left[c], 0.0)


def sides(left, right, fars, lefts, rights):
    high = bit(2)
    other = whole_of(fars)
    other = split(jnp.where(bit(1), other, other.T))

    @pl.when(high)
    def _():
        rights[...] = right[...]
        for c in range(lefts.shape[0]):
            lefts[c] = multiply(other, split(left[c]))

    @pl.when(jnp.logical_not(high))
    def _():
        lefts[...] = left[...]
        for c in range(lefts.shape[0]):
            rights[c] = multiply(split(right[c]), other)


def sides_kernel(n, left, right, *refs):
    sides(left, right, refs[:n], *refs[n:])


def level_kernel(k, whole, left, right, x, whole_out, left_out, right_out):
    after = bit(k)
    whole, left, right, x = whole[...], left[...], right[...], x[...]
    one = eye(whole.shape[0])
    whole_out[...] = product(jnp.where(after, x, whole), jnp.where(after, whole, x))
    for c in range(left.shape[0]):
        left_out[c] = product(jnp.where(after, x, one), left[c])
        right_out[c] = product(right[c], jnp.where(after, one, x))


def prepare(k, sent, lefts, rights, norm_out, a_out, b_out):
    y, transposed = split(sent[...]), split(sent[...].T)
    norm_out[...] = multiply(transposed, y)

    @pl.when(bit(k))
    def _():
        for c in range(lefts.shape[0]):
            a_out[c, 0], a_out[c, 1] = split(lefts[c])
            b_out[c, 0], b_out[c, 1] = split(multiply(split(rights[c]), y))

    @pl.when(jnp.logical_not(bit(k)))
    def _():
        for c in range(lefts.shape[0]):
            a_out[c, 0], a_out[c, 1] = split(multiply(transposed, split(lefts[c])))
            b_out[c, 0], b_out[c, 1] = split(rights[c])


def prepare_quad_kernel(n, k, sent, left, right, *refs):
    fars, (lefts, *outs), rights = refs[:n], refs[n:-1], refs[-1]
    sides(left, right, fars, lefts, rights)
    prepare(k, sent, lefts, rights, *outs)


def prepare_kernel(k, sent, left, right, lefts, *outs):
    lefts[...] = left[...]
    prepare(k, sent, lefts, right, *outs)


def terms_kernel(a, b, hamiltonian, out):
    for c in range(out.shape[0]):
        for t in range(out.shape[1]):
            inner = multiply((a[c, 0], a[c, 1]), split(hamiltonian[c, t, 0]))
            out[c, t] = multiply(split(inner), (b[c, 0], b[c, 1]))


def finish_kernel(share, passed, rest, terms, norm, out, x):
    rows = share.shape[0]
    at = bit(1).astype(jnp.int32) * rows
    x[pl.ds(pl.multiple_of(at, 8), rows)] = share[...]
    x[pl.ds(pl.multiple_of(rows - at, 8), rows)] = passed[...]
    x[2 * rows :] = rest[...]
    z = product(x[...].T, x[...])
    columns, count = terms.shape[0], terms.shape[1]

    def total(m):
        s = jnp.sum(z * m, axis=0, keepdims=True)
        return sum(s[:, i : i + LANES] for i in range(0, s.shape[1], LANES))

    sums = [total(terms[c, t]) for c in range(columns) for t in range(count)] + [total(norm[...])]
    sums += [jnp.zeros_like(sums[0])] * (out.shape[0] - len(sums))
    out[...] = jnp.concatenate(sums, axis=0)


def left_kernel(k, x, lefts, out):
    @pl.when(bit(k))
    def _():
        xs = split(x[...])
        for c in range(out.shape[0]):
            out[c, 0] = multiply(xs, split(lefts[c]))

    @pl.when(jnp.logical_not(bit(k)))
    def _():
        out[:, 0] = lefts[...]


def energy_kernel(scale, *refs):
    parts, out = [refs[0][...]] + [r[...] for r in refs[-2:0:-1]], refs[-1]
    while len(parts) > 1:
        parts = [a + b for a, b in zip(parts[::2], parts[1::2])]
    columns, terms = out.shape
    s = jnp.sum(parts[0], axis=1, keepdims=True)
    s = jnp.broadcast_to(scale * s / s[columns * terms : columns * terms + 1], parts[0].shape)
    row = lax.broadcasted_iota(jnp.int32, s.shape, 0)
    lane = lax.broadcasted_iota(jnp.int32, s.shape, 1)
    for c in range(columns):
        out[c : c + 1] = jnp.sum(jnp.where(row == c * terms + lane, s, 0.0), axis=0, keepdims=True)[:, :terms]


def call(kernel, outs, flops, *args, scratch=()):
    return pl.pallas_call(
        kernel,
        out_shape=outs,
        in_specs=[VMEM] * len(args),
        out_specs=jax.tree.map(lambda _: VMEM, outs),
        scratch_shapes=list(scratch),
        compiler_params=pltpu.CompilerParams(vmem_limit_bytes=LIMIT),
        cost_estimate=pl.CostEstimate(flops=flops, bytes_accessed=1 << 20, transcendentals=0),
    )(*args)


def per_device(transfer, hamiltonian, kept):
    columns, width, terms = transfer.shape[0], transfer.shape[2], hamiltonian.shape[1]
    total, sectors = lax.axis_size("col"), lax.axis_size("sec")
    half = total // 2
    one = 6 * width**3

    def array(*shape, dtype=F32):
        return jax.ShapeDtypeStruct(shape, dtype)

    matrix = array(width, width)
    room = (pltpu.VMEM((width, width), F32),)

    def swap(a, k):
        return lax.ppermute(a, "col", [(i, i ^ k) for i in range(total)])

    first = width * 21 // 256 * 8
    heights = [first, width - first]
    n = len(heights)
    whole, *parts = call(group_kernel, (matrix,) + tuple(array(h, width) for h in heights), one, transfer)
    turned = call(turn_kernel, array(2, width, width, dtype=BF16), one // 4, whole)
    nears = [swap(part, 1) for part in parts]
    pairs, fars = [], []
    for near, h in zip(nears, heights):
        pairs.append(call(pair_kernel, array(h, width), one // n, near, turned))
        fars.append(swap(pairs[-1], 2))
    both = array(columns, width, width)
    left, right = call(lambda *refs: near_kernel(n, *refs), (both, both), 2 * one, kept, transfer, *nears)
    fars[0], left = lax.optimization_barrier((fars[0], left))
    begun = call(lambda *refs: begin_kernel(n, *refs), matrix, one, *pairs, *fars[:-1])
    rows = width * 7 // 256 * 8
    shared = (matrix, array(rows, width), array(width - 2 * rows, width))
    if total <= 8:
        sent, share, rest = call(
            lambda *refs: quad_sent_kernel(n, half, *refs), shared, one, begun, *pairs, fars[-1], scratch=room
        )
    else:
        whole = call(lambda *refs: quad_kernel(n, *refs), matrix, one, begun, *pairs, fars[-1], scratch=room)
        left, right = call(lambda *refs: sides_kernel(n, *refs), (both, both), 2 * one, left, right, *fars)
        k = 4
        while k < half:
            x = swap(whole, k)
            whole, left, right = call(
                lambda *refs, k=k: level_kernel(k, *refs), (matrix, both, both), 5 * one, whole, left, right, x
            )
            k *= 2
        sent, share, rest = call(lambda *refs: sent_kernel(half, *refs), shared, one, whole)
    share = swap(share, half | 2)
    rest = swap(rest, half)
    halves = array(columns, 2, width, width, dtype=BF16)
    prepared = (array(columns, width, width), matrix, halves, halves)
    if total <= 8:
        lefts, norm, a, b = call(
            lambda *refs: prepare_quad_kernel(n, half, *refs), prepared, 5 * one, sent, left, right, *fars,
            scratch=(pltpu.VMEM((columns, width, width), F32),),
        )
    else:
        lefts, norm, a, b = call(
            lambda *refs: prepare_kernel(half, *refs), prepared, 3 * one, sent, left, right
        )
    passed = swap(share, 1)
    products = call(terms_kernel, array(columns, terms, width, width), 12 * one, a, b, hamiltonian)
    table_rows = -(-(columns * terms + 1) // 8) * 8
    table, x = call(
        finish_kernel, (array(table_rows, LANES), matrix), 2 * one, share, passed, rest, products, norm
    )
    parts = [table] + [lax.ppermute(table, "sec", [(i, i ^ k) for i in range(sectors)]) for k in range(sectors - 1, 0, -1)]
    left_env = call(
        lambda *refs: left_kernel(half, *refs), array(columns, 1, width, width), 2 * one, x, lefts
    )
    scale = float(width * sectors)
    energy = call(lambda *refs: energy_kernel(scale, *refs), array(columns, terms), 1000, *parts)
    return left_env, energy


def solution(mesh):
    in_specs = (P("col", "sec", None, None), P("col", None, "sec", None, None), P("col", "sec"))
    out_specs = (P("col", "sec", None, None), P("col", None))
    return jax.shard_map(
        per_device, mesh=mesh, in_specs=in_specs, out_specs=out_specs, check_vma=False
    )
```

```python
import jax
import jax.numpy as jnp
from jax import lax
from jax.experimental import pallas as pl
from jax.experimental.pallas import tpu as pltpu
from jax.sharding import PartitionSpec as P

F32 = jnp.float32
BF16 = jnp.bfloat16
VMEM = pl.BlockSpec(memory_space=pltpu.VMEM)
LIMIT = 40 * 1024 * 1024
LANES = 128


def split(a):
    high = a.astype(BF16)
    return high, (a - high.astype(F32)).astype(BF16)


def dot(a, b, over):
    return lax.dot_general(a, b, (over, ((), ())), preferred_element_type=F32)


def multiply(a, b, over=((1,), (0,))):
    return dot(a[0], b[0], over) + (dot(a[0], b[1], over) + dot(a[1], b[0], over))


def product(a, b):
    return multiply(split(a), split(b))


def bit(k):
    return (lax.axis_index("col") // k) % 2 == 1


def eye(width):
    rows = lax.broadcasted_iota(jnp.int32, (width, width), 0)
    return (rows == lax.broadcasted_iota(jnp.int32, (width, width), 1)).astype(F32)


def group_kernel(transfer, whole, *parts):
    group = transfer[0, 0]
    for c in range(1, transfer.shape[0]):
        group = product(group, transfer[c, 0])

    @pl.when(bit(1))
    def _():
        whole[...] = group.T

    @pl.when(jnp.logical_not(bit(1)))
    def _():
        whole[...] = group

    at = 0
    for part in parts:
        part[...] = whole[at : at + part.shape[0]]
        at += part.shape[0]


def turn_kernel(whole, turned):
    turned[0], turned[1] = split(whole[...].T)


def pair_kernel(near, turned, out):
    out[...] = multiply(split(near[...]), (turned[0], turned[1]))


def whole_of(parts):
    return jnp.concatenate([part[...] for part in parts], axis=0)


def begin_kernel(n, *refs):
    pairs, fars, out = refs[:n], refs[n:-1], refs[-1]
    pair, far = whole_of(pairs), whole_of(fars)
    rows = far.shape[0]

    @pl.when(bit(1) == bit(2))
    def _():
        out[:rows] = product(far, pair)
        out[rows:] = jnp.zeros_like(out[rows:])

    @pl.when(bit(1) != bit(2))
    def _():
        out[...] = product(pair[:, :rows], far)


def end_quad(begun, pairs, far, room):
    pair, far = whole_of(pairs), far[...]
    at = pair.shape[0] - far.shape[0]

    @pl.when(bit(1) == bit(2))
    def _():
        room[:at] = begun[:at]
        room[at:] = product(far, pair)

    @pl.when(bit(1) != bit(2))
    def _():
        room[...] = begun[...] + product(pair[:, at:], far)

    return room[...]


def quad_kernel(n, begun, *refs):
    pairs, (far, whole, room) = refs[:n], refs[n:]
    value = end_quad(begun, pairs, far, room)
    whole[...] = jnp.where(bit(1), value, value.T)


def spread(value, flip, sent, share, rest):
    @pl.when(flip)
    def _():
        sent[...] = value.T

    @pl.when(jnp.logical_not(flip))
    def _():
        sent[...] = value

    rows = share.shape[0]
    share[...] = sent[pl.ds(pl.multiple_of(bit(1).astype(jnp.int32) * rows, 8), rows)]
    rest[...] = sent[2 * rows :]


def quad_sent_kernel(n, k, begun, *refs):
    pairs, (far, sent, share, rest, room) = refs[:n], refs[n:]
    spread(end_quad(begun, pairs, far, room), bit(1) == bit(k), sent, share, rest)


def sent_kernel(k, whole, sent, share, rest):
    spread(whole[...], bit(k), sent, share, rest)


def near_kernel(n, kept, transfer, *refs):
    nears, (left, right) = refs[:n], refs[n:]
    last = transfer.shape[0] - 1
    near = whole_of(nears)

    @pl.when(bit(1))
    def _():
        left[0] = near
        for c in range(last):
            left[c + 1] = product(left[c], transfer[c, 0])
        right[last] = eye(near.shape[0])
        if last > 0:
            right[last - 1] = transfer[last, 0]
        for c in range(last - 2, -1, -1):
            right[c] = product(transfer[c + 1, 0], right[c + 1])

    @pl.when(jnp.logical_not(bit(1)))
    def _():
        left[0] = eye(near.shape[0])
        if last > 0:
            left[1] = transfer[0, 0]
        for c in range(1, last):
            left[c + 1] = product(left[c], transfer[c, 0])
        right[last] = near.T
        for c in range(last - 1, -1, -1):
            right[c] = product(transfer[c + 1, 0], right[c + 1])

    column = lax.broadcasted_iota(jnp.int32, near.shape, 1)
    for c in range(last + 1):
        left[c] = jnp.where(column < kept[c : c + 1], left[c], 0.0)


def sides(left, right, fars, lefts, rights):
    high = bit(2)
    other = whole_of(fars)
    other = split(jnp.where(bit(1), other, other.T))

    @pl.when(high)
    def _():
        rights[...] = right[...]
        for c in range(lefts.shape[0]):
            lefts[c] = multiply(other, split(left[c]))

    @pl.when(jnp.logical_not(high))
    def _():
        lefts[...] = left[...]
        for c in range(lefts.shape[0]):
            rights[c] = multiply(split(right[c]), other)


def sides_kernel(n, left, right, *refs):
    sides(left, right, refs[:n], *refs[n:])


def level_kernel(k, whole, left, right, x, whole_out, left_out, right_out):
    after = bit(k)
    whole, left, right, x = whole[...], left[...], right[...], x[...]
    one = eye(whole.shape[0])
    whole_out[...] = product(jnp.where(after, x, whole), jnp.where(after, whole, x))
    for c in range(left.shape[0]):
        left_out[c] = product(jnp.where(after, x, one), left[c])
        right_out[c] = product(right[c], jnp.where(after, one, x))


def prepare(k, sent, lefts, rights, norm_out, a_out, b_out):
    y, transposed = split(sent[...]), split(sent[...].T)
    norm_out[...] = multiply(transposed, y)

    @pl.when(bit(k))
    def _():
        for c in range(lefts.shape[0]):
            a_out[c, 0], a_out[c, 1] = split(lefts[c])
            b_out[c, 0], b_out[c, 1] = split(multiply(split(rights[c]), y))

    @pl.when(jnp.logical_not(bit(k)))
    def _():
        for c in range(lefts.shape[0]):
            a_out[c, 0], a_out[c, 1] = split(multiply(transposed, split(lefts[c])))
            b_out[c, 0], b_out[c, 1] = split(rights[c])


def prepare_quad_kernel(n, k, sent, left, right, *refs):
    fars, (lefts, *outs), rights = refs[:n], refs[n:-1], refs[-1]
    sides(left, right, fars, lefts, rights)
    prepare(k, sent, lefts, rights, *outs)


def prepare_kernel(k, sent, left, right, lefts, *outs):
    lefts[...] = left[...]
    prepare(k, sent, lefts, right, *outs)


def terms_kernel(a, b, hamiltonian, out):
    for c in range(out.shape[0]):
        for t in range(out.shape[1]):
            inner = multiply((a[c, 0], a[c, 1]), split(hamiltonian[c, t, 0]))
            out[c, t] = multiply(split(inner), (b[c, 0], b[c, 1]))


def finish_kernel(share, passed, rest, terms, norm, out, x):
    rows = share.shape[0]
    at = bit(1).astype(jnp.int32) * rows
    x[pl.ds(pl.multiple_of(at, 8), rows)] = share[...]
    x[pl.ds(pl.multiple_of(rows - at, 8), rows)] = passed[...]
    x[2 * rows :] = rest[...]
    z = product(x[...].T, x[...])
    columns, count = terms.shape[0], terms.shape[1]

    def total(m):
        s = jnp.sum(z * m, axis=0, keepdims=True)
        return sum(s[:, i : i + LANES] for i in range(0, s.shape[1], LANES))

    sums = [total(terms[c, t]) for c in range(columns) for t in range(count)] + [total(norm[...])]
    sums += [jnp.zeros_like(sums[0])] * (out.shape[0] - len(sums))
    out[...] = jnp.concatenate(sums, axis=0)


def left_kernel(k, x, lefts, out):
    @pl.when(bit(k))
    def _():
        xs = split(x[...])
        for c in range(out.shape[0]):
            out[c, 0] = multiply(xs, split(lefts[c]))

    @pl.when(jnp.logical_not(bit(k)))
    def _():
        out[:, 0] = lefts[...]


def energy_kernel(scale, *refs):
    parts, out = [refs[0][...]] + [r[...] for r in refs[-2:0:-1]], refs[-1]
    while len(parts) > 1:
        parts = [a + b for a, b in zip(parts[::2], parts[1::2])]
    columns, terms = out.shape
    s = jnp.sum(parts[0], axis=1, keepdims=True)
    s = jnp.broadcast_to(scale * s / s[columns * terms : columns * terms + 1], parts[0].shape)
    row = lax.broadcasted_iota(jnp.int32, s.shape, 0)
    lane = lax.broadcasted_iota(jnp.int32, s.shape, 1)
    for c in range(columns):
        out[c : c + 1] = jnp.sum(jnp.where(row == c * terms + lane, s, 0.0), axis=0, keepdims=True)[:, :terms]


def call(kernel, outs, flops, *args, scratch=()):
    return pl.pallas_call(
        kernel,
        out_shape=outs,
        in_specs=[VMEM] * len(args),
        out_specs=jax.tree.map(lambda _: VMEM, outs),
        scratch_shapes=list(scratch),
        compiler_params=pltpu.CompilerParams(vmem_limit_bytes=LIMIT),
        cost_estimate=pl.CostEstimate(flops=flops, bytes_accessed=1 << 20, transcendentals=0),
    )(*args)


def per_device(transfer, hamiltonian, kept):
    columns, width, terms = transfer.shape[0], transfer.shape[2], hamiltonian.shape[1]
    total, sectors = lax.axis_size("col"), lax.axis_size("sec")
    half = total // 2
    one = 6 * width**3

    def array(*shape, dtype=F32):
        return jax.ShapeDtypeStruct(shape, dtype)

    matrix = array(width, width)
    room = (pltpu.VMEM((width, width), F32),)

    def swap(a, k):
        return lax.ppermute(a, "col", [(i, i ^ k) for i in range(total)])

    first = width * 21 // 256 * 8
    heights = [first, width - first]
    n = len(heights)
    whole, *parts = call(group_kernel, (matrix,) + tuple(array(h, width) for h in heights), one, transfer)
    turned = call(turn_kernel, array(2, width, width, dtype=BF16), one // 4, whole)
    nears = [swap(part, 1) for part in parts]
    pairs, fars = [], []
    for near, h in zip(nears, heights):
        pairs.append(call(pair_kernel, array(h, width), one // n, near, turned))
        fars.append(swap(pairs[-1], 2))
    both = array(columns, width, width)
    left, right = call(lambda *refs: near_kernel(n, *refs), (both, both), 2 * one, kept, transfer, *nears)
    fars[0], left = lax.optimization_barrier((fars[0], left))
    begun = call(lambda *refs: begin_kernel(n, *refs), matrix, one, *pairs, *fars[:-1])
    rows = width // 4
    shared = (matrix, array(rows, width), array(width - 2 * rows, width))
    if total <= 8:
        sent, share, rest = call(
            lambda *refs: quad_sent_kernel(n, half, *refs), shared, one, begun, *pairs, fars[-1], scratch=room
        )
    else:
        whole = call(lambda *refs: quad_kernel(n, *refs), matrix, one, begun, *pairs, fars[-1], scratch=room)
        left, right = call(lambda *refs: sides_kernel(n, *refs), (both, both), 2 * one, left, right, *fars)
        k = 4
        while k < half:
            x = swap(whole, k)
            whole, left, right = call(
                lambda *refs, k=k: level_kernel(k, *refs), (matrix, both, both), 5 * one, whole, left, right, x
            )
            k *= 2
        sent, share, rest = call(lambda *refs: sent_kernel(half, *refs), shared, one, whole)
    share = swap(share, half | 2)
    rest = swap(rest, half)
    halves = array(columns, 2, width, width, dtype=BF16)
    prepared = (array(columns, width, width), matrix, halves, halves)
    if total <= 8:
        lefts, norm, a, b = call(
            lambda *refs: prepare_quad_kernel(n, half, *refs), prepared, 5 * one, sent, left, right, *fars,
            scratch=(pltpu.VMEM((columns, width, width), F32),),
        )
    else:
        lefts, norm, a, b = call(
            lambda *refs: prepare_kernel(half, *refs), prepared, 3 * one, sent, left, right
        )
    passed = swap(share, 1)
    products = call(terms_kernel, array(columns, terms, width, width), 12 * one, a, b, hamiltonian)
    table_rows = -(-(columns * terms + 1) // 8) * 8
    table, x = call(
        finish_kernel, (array(table_rows, LANES), matrix), 2 * one, share, passed, rest, products, norm
    )
    parts = [table] + [lax.ppermute(table, "sec", [(i, i ^ k) for i in range(sectors)]) for k in range(sectors - 1, 0, -1)]
    left_env = call(
        lambda *refs: left_kernel(half, *refs), array(columns, 1, width, width), 2 * one, x, lefts
    )
    scale = float(width * sectors)
    energy = call(lambda *refs: energy_kernel(scale, *refs), array(columns, terms), 1000, *parts)
    return left_env, energy


def solution(mesh):
    in_specs = (P("col", "sec", None, None), P("col", None, "sec", None, None), P("col", "sec"))
    out_specs = (P("col", "sec", None, None), P("col", None))
    return jax.shard_map(
        per_device, mesh=mesh, in_specs=in_specs, out_specs=out_specs, check_vma=False
    )
```
